256 devices in a mesh: interval: 4 (over y), sample: 64 (over x, z, core).
Axes of the slice: x: 4, y: 4, z: 8, core: 2. Of those that a mesh axis runs over, the one named last changes fastest.
Arguments:
- probes: bfloat16 [65536, 128], P('sample'), may hold values from -6 to 6
- lengths: float32 [4, 4096], P('interval'), may hold values from 0.1 to 10
- incidence: bfloat16 [4, 32768, 64, 128], P('interval', 'sample'), may hold values from -6 to 6
- block_rows: int32 [4, 32768], P('interval', 'sample'), may hold values from 0 to 7
- block_cols: int32 [4, 32768], P('interval', 'sample'), may hold values from 0 to 63
- block_count: int32 [4, 64], P('interval', 'sample'), may hold values from 102 to 512, as said below
- tree_sample: int32 [65536], P('sample'), may hold values from 0 to 65535, as said below
- tree_position: int32 [65536], P('sample'), may hold values from 0 to 65535, as said below
Outputs:
- basis: float32 [65536, 128], P('sample')
- triangle: float32 [128, 128], replicated
The draws below stay inside these ranges and needn't reach their ends.
Inputs may be any that keep to these rules, and one draw needn't show every extreme that they name: `block_count`: one device of every group has all 512 slots live. `tree_sample`: a permutation of the samples; every aligned block of 1024 tree positions holds exactly 16 samples of every aligned block of 1024 samples. `tree_position`: the inverse permutation of tree_sample.
All inputs are finite; a program needn't handle non-finite values.
Results may differ from the reference program's by a relative error of at most 0.0039.
Values may be sent and summed in bfloat16 or wider, within the bound.
No kernel may reach another device: no remote copies, remote signals or barrier semaphores. Data moves between devices by JAX's collectives and lax.ppermute only.
A program may use at most 64 MiB of HBM per device.

```python
import math
import jax
import jax.numpy as jnp
from jax import lax

PROBES = 128
BLOCK_SAMP = 128
BLOCK_NODES = 64
SAMP_DEV = 1024
BLK_DEV = 512
ITERS = 2
GROUPS = 4
SAMPLES = 65536
NODES = 4096
BLOCKS = 32768
N_SAMPLE = 64


def tree_pair(key):
    ndev = SAMPLES // SAMP_DEV
    share = SAMP_DEV // ndev
    key_src, key_dst = jax.random.split(key)
    source_perm = jax.vmap(lambda k: jax.random.permutation(k, SAMP_DEV))(jax.random.split(key_src, ndev))
    offsets = (jnp.arange(ndev, dtype=jnp.int32) * SAMP_DEV)[:, None, None]
    listed = source_perm.reshape(ndev, ndev, share).astype(jnp.int32) + offsets
    listed = jnp.transpose(listed, (1, 0, 2)).reshape(ndev, SAMP_DEV)
    shuffle = jax.vmap(lambda k: jax.random.permutation(k, SAMP_DEV))(jax.random.split(key_dst, ndev))
    sample_at = jnp.take_along_axis(listed, shuffle.astype(jnp.int32), axis=1).reshape(-1).astype(jnp.int32)
    position_of = jnp.zeros((SAMPLES,), jnp.int32).at[sample_at].set(jnp.arange(SAMPLES, dtype=jnp.int32))
    return (sample_at, position_of)


def draw_tree_sample(key, part):
    return tree_pair(key)[0]


def draw_tree_position(key, part):
    return tree_pair(key)[1]


def draw_block_count(key, part):
    key = jax.random.fold_in(key, 11)
    key_load, key_top = jax.random.split(key)
    ndev = SAMPLES // SAMP_DEV
    low = BLK_DEV // 5
    draws = jax.random.randint(key_load, (GROUPS, ndev), 0, 257)
    counts = low + draws * draws * (BLK_DEV - low) // 65536
    fullest = jax.random.randint(key_top, (GROUPS, 1), 0, ndev)
    counts = jnp.where(jnp.arange(ndev)[None, :] == fullest, BLK_DEV, counts)
    return counts.astype(jnp.int32)


def with_ends(values, rng, least, largest):
    index_at = [jax.random.randint(jax.random.fold_in(rng, axis), (), 0, length) for axis, length in enumerate(values.shape)]
    main_axis = values.shape.index(max(values.shape))
    next_to = index_at[:main_axis] + [(index_at[main_axis] + 1) % values.shape[main_axis]] + index_at[main_axis + 1:]
    return values.at[tuple(index_at)].set(least).at[tuple(next_to)].set(largest)


def steps_of(key, dims, shards, smallest, top_value):
    loudness = 1.0
    for dim, blocks in shards:
        steps = jax.random.uniform(jax.random.fold_in(jax.random.fold_in(key, 6), dim), (blocks,), jnp.float32, smallest / len(shards), top_value / len(shards))
        loudness = loudness * jnp.repeat(jnp.exp(steps), dims[dim] // blocks).reshape((-1,) + (1,) * (len(dims) - 1 - dim))
    return loudness


def bell_draw(stream_key, extent, spread, bound, pieces=(), kind=jnp.bfloat16):
    values = spread * jax.random.normal(stream_key, extent, jnp.float32)
    if pieces:
        values = values * steps_of(stream_key, extent, pieces, -0.22, 0.18)
    return jnp.clip(values, -bound, bound).astype(kind)


def setup_inputs(seed: int = 0) -> dict:
    key_of = jax.random.split(jax.random.key(seed), 9)
    probes = bell_draw(key_of[0], (SAMPLES, PROBES), 1.0, 6.0, ((0, 64),))
    lengths = jnp.clip(jnp.exp(math.log(10.0) - 4.6051702 * jax.random.uniform(key_of[1], (GROUPS, NODES), jnp.float32) ** steps_of(key_of[1], (GROUPS, NODES), ((0, 4),), -0.2, 0.2)), 0.1, 10.0)
    incidence = bell_draw(key_of[2], (GROUPS, BLOCKS, BLOCK_NODES, BLOCK_SAMP), 1.0, 6.0, ((0, 4), (1, 64)))
    block_rows = with_ends(jax.random.randint(key_of[3], (GROUPS, BLOCKS), 0, SAMP_DEV // BLOCK_SAMP), jax.random.fold_in(key_of[3], 1), 0, (SAMP_DEV // BLOCK_SAMP) - 1).astype(jnp.int32)
    block_cols = with_ends(jax.random.randint(key_of[4], (GROUPS, BLOCKS), 0, N_SAMPLE), jax.random.fold_in(key_of[4], 1), 0, N_SAMPLE - 1).astype(jnp.int32)
    block_count = draw_block_count(jax.random.fold_in(key_of[8], 71), 0)
    tree_sample = draw_tree_sample(jax.random.fold_in(key_of[8], 71), 0)
    tree_position = draw_tree_position(jax.random.fold_in(key_of[8], 71), 0)
    return {"probes": probes, "lengths": lengths, "incidence": incidence, "block_rows": block_rows, "block_cols": block_cols, "block_count": block_count, "tree_sample": tree_sample, "tree_position": tree_position}


def image_of(probe_tree, lengths, incidence, block_rows, block_cols, block_count):
    samples = probe_tree.shape[0]
    ndev = samples // SAMP_DEV
    rbd = SAMP_DEV // BLOCK_SAMP
    row_blocks = probe_tree.reshape(samples // BLOCK_SAMP, BLOCK_SAMP, PROBES).astype(jnp.float32)
    slots = jnp.arange(BLK_DEV, dtype=jnp.int32)
    devices = jnp.arange(ndev, dtype=jnp.int32)
    total = jnp.zeros((samples, PROBES), jnp.float32)
    for group in range(GROUPS):
        blocks = incidence[group].reshape(ndev, BLK_DEV, BLOCK_NODES, BLOCK_SAMP)
        rows = block_rows[group].reshape(ndev, BLK_DEV)
        cols = block_cols[group].reshape(ndev, BLK_DEV)
        counts = block_count[group]

        def node_step(carry, items):
            blk, row, col, cnt, dev = items
            live = (slots < cnt).astype(jnp.float32)
            picked = row_blocks[dev * rbd + row]
            prod = jnp.einsum('bns,bsp->bnp', blk.astype(jnp.float32), picked, precision=lax.Precision.HIGHEST)
            prod = prod * live[:, None, None]
            return (carry + jax.ops.segment_sum(prod, col, num_segments=ndev), None)
        node_sum, _ = lax.scan(node_step, jnp.zeros((ndev, BLOCK_NODES, PROBES), jnp.float32), (blocks, rows, cols, counts, devices))
        node_weight = (lengths[group].reshape(ndev, BLOCK_NODES)[:, :, None] * node_sum / samples).astype(jnp.bfloat16)

        def image_step(items):
            blk, row, col, cnt = items
            live = (slots < cnt).astype(jnp.float32)
            picked = node_weight[col].astype(jnp.float32)
            prod = jnp.einsum('bns,bnp->bsp', blk.astype(jnp.float32), picked, precision=lax.Precision.HIGHEST)
            prod = prod * live[:, None, None]
            return jax.ops.segment_sum(prod, row, num_segments=rbd).reshape(SAMP_DEV, PROBES)
        part = lax.map(image_step, (blocks, rows, cols, counts))
        total = total + part.reshape(samples, PROBES)
    return total

def reference(probes, lengths, incidence, block_rows, block_cols, block_count, tree_sample, tree_position):
    samples = probes.shape[0]
    root = math.sqrt(samples)
    probe = probes
    identity = jnp.eye(PROBES, dtype=jnp.float32)
    for step in range(ITERS):
        tree_probe = probe[tree_sample]
        tree_image = image_of(tree_probe, lengths, incidence, block_rows, block_cols, block_count)
        image = tree_image[tree_position]
        gram = jnp.dot(image.T.astype(jnp.float32), image.astype(jnp.float32), precision=lax.Precision.HIGHEST, preferred_element_type=jnp.float32)
        lower = jnp.linalg.cholesky(gram)
        inverse = lax.linalg.triangular_solve(lower, identity, left_side=True, lower=True)
        basis = root * jnp.dot(image.astype(jnp.float32), inverse.T.astype(jnp.float32), precision=lax.Precision.HIGHEST, preferred_element_type=jnp.float32)
        probe = basis.astype(jnp.bfloat16)
    return (basis, lower.T / root)
```

```python
import functools
import math

import jax
import jax.numpy as jnp
from jax import lax
from jax.experimental import pallas as pl
from jax.experimental.pallas import tpu as pltpu
from jax.sharding import PartitionSpec as P

ITERS = 2
X, Z, C = 4, 8, 2
HIGH = lax.Precision.HIGHEST
F32 = jnp.float32
BF16 = jnp.bfloat16
MIB = 1024 * 1024
I16 = jnp.int16
QUARTERS = 4
TILE = 512


def dense_kernel(order_ref, node_ref, lane_ref, keep_ref, bound_ref, blk_ref, out_ref, held, z, sem):
    nodes, rows = z.shape
    nbk, sb = held.shape[1:]
    tile = 128
    copy = pltpu.make_async_copy(blk_ref, held, sem.at[0])
    copy.start()

    def zero(i, carry):
        z[pl.ds(pl.multiple_of(i * tile, tile), tile), :] = jnp.zeros((tile, rows), BF16)
        return carry

    lax.fori_loop(0, nodes // tile, zero, 0)
    copy.wait()

    def add(i, total):
        total = jnp.where(keep_ref[i] == 1, total, 0.0) + held[order_ref[i]].astype(F32)
        node = pl.multiple_of(node_ref[i], nbk)
        lane = pl.multiple_of(lane_ref[i], sb)
        z[pl.ds(node, nbk), pl.ds(lane, sb)] = total.astype(BF16)
        return total

    unroll = 8
    total = jnp.zeros((nbk, sb), F32)
    part = nodes // QUARTERS
    backs = []
    for q in range(QUARTERS):
        first = 0 if q == 0 else bound_ref[q - 1]
        last = bound_ref[q]
        turns = (last - first) // unroll

        def several(i, total, first=first):
            for j in range(unroll):
                total = add(first + i * unroll + j, total)
            return total

        total = lax.fori_loop(0, turns, several, total)
        total = lax.fori_loop(first + turns * unroll, last, add, total)
        at = pl.ds(q * part, part)
        backs.append(pltpu.make_async_copy(z.at[at], out_ref.at[at], sem.at[1 + q]))
        backs[-1].start()
    for back in backs:
        back.wait()


def dense(blocks, row_at, col_at, count, nodes, rows):
    slots, nbk, sb = blocks.shape
    nrow = rows // sb
    place = col_at * nrow + row_at
    at = jnp.arange(slots, dtype=jnp.int32)
    live = at < count[0]
    key = jnp.where(live, place * slots, nodes * rows) + at
    rank = jnp.sum((key[None, :] < key[:, None]).astype(jnp.int32), axis=1)
    earlier = (place[None, :] == place[:, None]) & (at[None, :] < at[:, None])
    keep = jnp.max(earlier.astype(jnp.int32), axis=1)
    hit = rank[None, :] == at[:, None]
    order, node, lane, keep = [
        jnp.sum(jnp.where(hit, value[None, :], 0), axis=1)
        for value in (at, col_at * nbk, row_at * sb, keep)
    ]
    ends = (jnp.arange(QUARTERS, dtype=jnp.int32) + 1) * (nodes // nbk * nrow // QUARTERS)
    bound = jnp.sum((live & (place < ends[:, None])).astype(jnp.int32), axis=1)
    return pl.pallas_call(
        dense_kernel,
        out_shape=pltpu.HBM((nodes, rows), BF16),
        in_specs=[pl.BlockSpec(memory_space=pltpu.SMEM)] * 5 + [pl.BlockSpec(memory_space=pl.ANY)],
        out_specs=pl.BlockSpec(memory_space=pl.ANY),
        scratch_shapes=[
            pltpu.VMEM(blocks.shape, BF16),
            pltpu.VMEM((nodes, rows), BF16),
            pltpu.SemaphoreType.DMA((1 + QUARTERS,)),
        ],
        compiler_params=pltpu.CompilerParams(vmem_limit_bytes=20 * MIB),
        name="dense",
    )(order, node, lane, keep, bound, pltpu.with_memory_space_constraint(blocks, pltpu.HBM))


def chol_kernel(a_ref, upper_ref, inv_ref):
    n = a_ref.shape[0]
    groups = n // 8
    block = 4
    lane = lax.broadcasted_iota(jnp.int32, (8, n), 1)
    sub = lax.broadcasted_iota(jnp.int32, (8, n), 0)
    a = [a_ref[g * 8 : g * 8 + 8, :] for g in range(groups)]
    x = [(lane == sub + g * 8).astype(F32) for g in range(groups)]

    def row(value, i):
        return jnp.broadcast_to(value[i : i + 1, :], (8, n))

    def column(value, k):
        return jnp.broadcast_to(value[:, k : k + 1], (8, n))

    for k in range(0, n, block):
        g0, s = divmod(k, 8)
        cols = [column(a[g0], k + j) for j in range(block)]
        m = [[row(cols[j], s + i) for j in range(i + 1)] for i in range(block)]
        ra = [row(a[g0], s + i) for i in range(block)]
        rx = [row(x[g0], s + i) for i in range(block)]
        low = {}
        for j in range(block):
            one = 1.0 / m[j][j]
            for i in range(j + 1, block):
                low[i, j] = m[i][j] * one
                for h in range(j + 1, i + 1):
                    m[i][h] = m[i][h] - low[i, j] * m[h][j]
                ra[i] = ra[i] - low[i, j] * ra[j]
                rx[i] = rx[i] - low[i, j] * rx[j]
            ra[j], rx[j] = ra[j] * one, rx[j] * one
        for g in range(g0, groups):
            if g > g0:
                cols = [column(a[g], k + j) for j in range(block)]
            c = list(cols)
            for j in range(block):
                for h in range(j):
                    c[j] = c[j] - c[h] * low[j, h]
            if g == g0:
                c = [jnp.where(sub > s + j, c[j], 0.0) for j in range(block)]
            for j in range(block):
                a[g] = a[g] - c[j] * ra[j]
                x[g] = x[g] - c[j] * rx[j]
    for g in range(groups):
        own = lane == sub + g * 8
        diag = jnp.sum(jnp.where(own, a[g], 0.0), axis=1, keepdims=True)
        inv_root = 1.0 / jnp.sqrt(diag)
        upper_ref[g * 8 : g * 8 + 8, :] = jnp.where(lane >= sub + g * 8, a[g] * inv_root, 0.0)
        inv_ref[g * 8 : g * 8 + 8, :] = x[g] * inv_root


def factor(gram):
    shape = jax.ShapeDtypeStruct(gram.shape, F32)
    return pl.pallas_call(
        chol_kernel,
        out_shape=(shape, shape),
        compiler_params=pltpu.CompilerParams(vmem_limit_bytes=4 * MIB),
        name="factor",
    )(gram)


def two_parts(value):
    high = value.astype(BF16)
    low = (value - high.astype(F32)).astype(BF16)
    return jnp.concatenate([high, low], axis=1)


def fetched(z_ref, held, sem, first):
    copies = []
    for i in range(held.shape[0] // TILE):
        source = z_ref.at[pl.ds(first + i * TILE, TILE)]
        copies.append(pltpu.make_async_copy(source, held.at[pl.ds(i * TILE, TILE)], sem.at[i]))
        copies[-1].start()
    return copies


def node_kernel(z_ref, p_ref, out_ref, held, sem, *both, first):
    width = out_ref.shape[1]
    copies = fetched(z_ref, held, sem, first)
    right = p_ref
    if both:
        right = both[0]
        right[...] = two_parts(p_ref[...])
    for i, copy in enumerate(copies):
        copy.wait()
        at = slice(i * TILE, (i + 1) * TILE)
        prod = jnp.dot(held[at, :], right[...], preferred_element_type=F32)
        total = prod[:, :width]
        if both:
            total = total + prod[:, width:]
        out_ref[at, :] = total


def node_half(dense_z, probe, part):
    nodes, rows = dense_z.shape
    width = probe.shape[1]
    half = nodes // C
    both = [] if probe.dtype == BF16 else [pltpu.VMEM((rows, 2 * width), BF16)]
    return pl.pallas_call(
        functools.partial(node_kernel, first=part * half),
        out_shape=jax.ShapeDtypeStruct((half, width), F32),
        in_specs=[
            pl.BlockSpec(memory_space=pl.ANY),
            pl.BlockSpec(memory_space=pltpu.VMEM),
        ],
        out_specs=pl.BlockSpec(memory_space=pltpu.VMEM),
        scratch_shapes=[
            pltpu.VMEM((half, rows), BF16),
            pltpu.SemaphoreType.DMA((half // TILE,)),
        ]
        + both,
        compiler_params=pltpu.CompilerParams(vmem_limit_bytes=12 * MIB),
        name="node_half",
    )(pltpu.with_memory_space_constraint(dense_z, pltpu.HBM), probe)


def image_kernel(z_ref, first_ref, second_ref, out_ref, held, sem, acc, *, nbk):
    width = out_ref.shape[1]
    copies = fetched(z_ref, held, sem, 0)
    each = TILE // nbk
    half = len(copies) // C
    for step, copy in enumerate(copies):
        w_ref = first_ref if step < half else second_ref
        at = step % half * each
        if w_ref.dtype == BF16:
            w = w_ref[at : at + each].reshape(TILE, width)
        else:
            parts = []
            for piece in range(at, at + each):
                code = w_ref[piece].astype(jnp.int32).astype(F32)
                parts.append(code[:nbk] * jnp.exp2(code[nbk : nbk + 1] - 14.0))
            w = two_parts(jnp.concatenate(parts, axis=0))
        copy.wait()
        z = held[step * TILE : (step + 1) * TILE, :]
        prod = lax.dot_general(w, z, (((0,), (0,)), ((), ())), preferred_element_type=F32)
        if step == 0:
            acc[...] = prod
        else:
            acc[...] += prod
    total = acc[:width, :]
    for i in range(width, acc.shape[0], width):
        total = total + acc[i : i + width, :]
    out_ref[...] = total.T


def image_part(dense_z, first, second, nbk):
    nodes, rows = dense_z.shape
    width = first.shape[2]
    parts = 1 if first.dtype == BF16 else 2
    return pl.pallas_call(
        functools.partial(image_kernel, nbk=nbk),
        out_shape=jax.ShapeDtypeStruct((rows, width), F32),
        in_specs=[
            pl.BlockSpec(memory_space=pl.ANY),
            pl.BlockSpec(memory_space=pltpu.VMEM),
            pl.BlockSpec(memory_space=pltpu.VMEM),
        ],
        out_specs=pl.BlockSpec(memory_space=pltpu.VMEM),
        scratch_shapes=[
            pltpu.VMEM((nodes, rows), BF16),
            pltpu.SemaphoreType.DMA((nodes // TILE,)),
            pltpu.VMEM((parts * width, rows), F32),
        ],
        compiler_params=pltpu.CompilerParams(vmem_limit_bytes=18 * MIB),
        name="image_part",
    )(pltpu.with_memory_space_constraint(dense_z, pltpu.HBM), first, second)


def along(axis, k):
    pairs = []
    for s in range(X * Z * C):
        x, z, c = s // (Z * C), s // C % Z, s % C
        if axis == "x":
            x = (x + k) % X
        if axis == "z":
            z = (z + k) % Z
        if axis == "c":
            c = (c + k) % C
        pairs.append((s, (x * Z + z) * C + c))
    return pairs


def from_core(value):
    return lax.ppermute(value, "sample", along("c", 1))


def exchange(value):
    groups = [[s for s in range(X * Z * C) if s % C == c] for c in range(C)]
    return lax.all_to_all(
        value, "sample", split_axis=0, concat_axis=0, axis_index_groups=groups, tiled=True
    )


def coded(value):
    top = jnp.max(jnp.abs(value), axis=1, keepdims=True)
    power = jnp.floor(jnp.log2(jnp.maximum(top, 1e-30))) + 1.0
    power = jnp.clip(power, -100.0, 127.0)
    return value * jnp.exp2(14.0 - power), power


def whole(value):
    return jnp.round(value).astype(I16)


def decoded(code, power):
    return code.astype(F32) * jnp.exp2(power.astype(F32) - 14.0)


def message(value, gram, lines):
    scaled, power = coded(value)
    rows = [whole(scaled), power.astype(I16)]
    if gram is not None:
        scaled, power = coded(gram)
        high = jnp.round(scaled)
        rows += [high.astype(I16), whole((scaled - high) * 2.0**14), power.astype(I16)]
    rows = jnp.concatenate(rows, axis=1)
    return jnp.pad(rows, ((0, 0), (0, lines - rows.shape[1]), (0, 0)))


def read_value(rows, own):
    return decoded(rows[:, :own], rows[:, own : own + 1])


def read_gram(rows, own, lines):
    at = own + 1
    code = rows[:, at : at + lines].astype(F32)
    code = code + rows[:, at + lines : at + 2 * lines].astype(F32) * 2.0**-14
    return decoded(code, rows[:, at + 2 * lines : at + 2 * lines + 1])


def sum_nodes(dense_z, probe, gram, others):
    nodes = dense_z.shape[0]
    width = probe.shape[1]
    lines = width // (X * Z * C)
    other = from_core(node_half(dense_z, probe, 1))
    if gram is not None:
        gram = (gram[0] + from_core(gram[1])).reshape(X * Z, lines, width)
    mine = (node_half(dense_z, probe, 0) + other).reshape(X * Z, -1, width)
    own = mine.shape[1]
    sent = message(mine, gram, own + 8)
    sent, others = lax.optimization_barrier((sent, others))
    got = exchange(sent.reshape(-1, width))
    got, others = lax.optimization_barrier((got, others))
    got = got.reshape(X * Z, -1, width)
    if gram is not None:
        gram = jnp.sum(read_gram(got, own, lines), axis=0)
    return jnp.sum(read_value(got, own), axis=0), gram, others


def spread(own, others):
    copies = jnp.broadcast_to(own[None], (X * Z,) + own.shape).reshape(-1, own.shape[1])
    copies, others = lax.optimization_barrier((copies, others))
    mine = exchange(copies)
    mine, others = lax.optimization_barrier((mine, others))
    mine = mine.reshape((X * Z,) + own.shape)
    return mine, from_core(mine), others


def scatter_interval(value, ny):
    piece = value.shape[0] // ny
    total = value[:piece]
    for k in range(1, ny):
        sent = value[k * piece : (k + 1) * piece]
        total = total + lax.ppermute(sent, "interval", [(i, (i + k) % ny) for i in range(ny)])
    return total


def gather_interval(value, ny):
    parts = [value]
    for k in range(1, ny):
        parts.append(lax.ppermute(value, "interval", [(i, (i - k) % ny) for i in range(ny)]))
    return jnp.concatenate(parts, axis=0)


def split(value, count):
    parts = []
    for _ in range(count):
        part = lax.reduce_precision(value, exponent_bits=8, mantissa_bits=7)
        value = value - part
        parts.append(part.astype(BF16))
    return jnp.concatenate(parts, axis=1)


def gram_of(image):
    return lax.dot_general(
        image, image, (((0,), (0,)), ((), ())), precision=HIGH, preferred_element_type=F32
    )


def shards(
    probes, lengths, incidence, block_rows, block_cols, block_count, tree_sample, tree_position
):
    ndev = lax.axis_size("sample")
    ny = lax.axis_size("interval")
    mine = lax.axis_index("sample")
    iy = lax.axis_index("interval")
    rows_here, width = probes.shape
    samples = rows_here * ndev
    root = math.sqrt(samples)
    share = rows_here // ndev
    quarter = rows_here // ny
    blocks = incidence[0]
    slots, nbk, sb = blocks.shape
    nodes = ndev * nbk
    nrow = rows_here // sb
    turn = nrow // ny

    at = jnp.arange(rows_here, dtype=jnp.int32)
    rank = jnp.sum((tree_position[None, :] < tree_position[:, None]).astype(jnp.int32), axis=1)
    to_send = (at[:, None] == rank[None, :]).astype(BF16)
    sent = jnp.dot(to_send, probes, preferred_element_type=F32).astype(BF16)
    moved = lax.all_to_all(sent, "sample", split_axis=0, concat_axis=0, tiled=True)

    source = tree_sample // rows_here
    same = (source[None, :] == source[:, None]) & (at[None, :] < at[:, None])
    order = jnp.sum(same.astype(jnp.int32), axis=1)
    source = jnp.roll(source, -iy * quarter)
    order = jnp.roll(order, -iy * quarter)
    slot = source * share + order
    from_moved = (slot[:, None] == at[None, :]).astype(BF16)
    tree_probe = jnp.dot(from_moved, moved, preferred_element_type=F32).astype(BF16)

    rows = block_rows[0]
    cols = block_cols[0]
    row_at = (rows + nrow - iy * turn) % nrow
    col_at = ((cols + mine) % C) * (ndev // C) + cols // C
    dense_z = dense(blocks, row_at, col_at, block_count[0], nodes, rows_here)
    half = nodes // C

    own_lens = lax.dynamic_slice_in_dim(lengths[0], mine * nbk, nbk, 0)

    def scale(owned):
        return own_lens[:, None] * owned / samples

    core = mine % C
    tied = (own_lens, rank, source, order, core)
    owned, _, tied = sum_nodes(dense_z, tree_probe, None, tied)
    own_lens, core = tied[0], tied[4]
    first, second, tied = spread(scale(owned).astype(BF16), tied)
    part = image_part(dense_z, first, second, nbk)
    image = gather_interval(scatter_interval(part, ny), ny)

    gram = jnp.split(gram_of(image), C, axis=0)
    gram = [jnp.where(core == c, gram[0], gram[1]) for c in range(C)]
    owned, gram, tied = sum_nodes(dense_z, image, gram, tied)
    own_lens = tied[0]
    first, second, tied = spread(message(scale(owned)[None], gram[None], nbk + 16)[0], tied)
    rank, source, order, core = tied[1:]
    lines = width // ndev
    gram = [read_gram(got, nbk, lines).reshape(-1, width) for got in (first, second)]
    gram = jnp.concatenate([jnp.where(core == c, gram[0], gram[1]) for c in range(C)], axis=0)
    _, inverse = factor(gram)
    part = image_part(dense_z, first, second, nbk)

    per = share // ny
    jrel = (order // per + ny - iy) % ny
    goal = jrel * quarter + source * per + order % per
    to_goal = (at[:, None] == goal[None, :]).astype(BF16)
    pieces = jnp.dot(to_goal, split(part, 3), preferred_element_type=F32)
    part = pieces[:, :width] + pieces[:, width : 2 * width] + pieces[:, 2 * width :]
    image = scatter_interval(part, ny)
    image = root * jnp.dot(image, inverse.T, precision=HIGH, preferred_element_type=F32)
    gram = gram_of(image).reshape(ndev, -1, width)
    image = jnp.concatenate([image.reshape(ndev, per, width), gram], axis=1)
    image = jnp.pad(image, ((0, 0), (0, -image.shape[1] % 8), (0, 0)))
    image, rank = lax.optimization_barrier((image, rank))
    image = lax.all_to_all(
        image.reshape(-1, width), "sample", split_axis=0, concat_axis=0, tiled=True
    )
    image, rank = lax.optimization_barrier((image, rank))
    image = image.reshape(ndev, -1, width)
    gram = jnp.sum(image[:, per : per + lines], axis=0)
    image = image[:, :per].reshape(quarter, width)
    gram = jnp.broadcast_to(gram[None], (ny * ndev,) + gram.shape).reshape(-1, width)
    gram, image, rank = lax.optimization_barrier((gram, image, rank))
    gram = lax.all_to_all(gram, ("interval", "sample"), split_axis=0, concat_axis=0, tiled=True)
    gram, image, rank = lax.optimization_barrier((gram, image, rank))
    gram = jnp.sum(gram.reshape(ny, width, width), axis=0)
    upper, inverse = factor(gram)
    basis = root * jnp.dot(image, inverse.T, precision=HIGH, preferred_element_type=F32)
    sent = jnp.pad(message(basis[None], None, quarter + 1)[0], ((0, 7), (0, 0)))
    basis = gather_interval(sent, ny).reshape(ny, -1, width)
    basis = split(read_value(basis, quarter).reshape(rows_here, width), 2)
    k = rank % share
    back = ((k // per + ny - iy) % ny) * quarter + (rank // share) * per + k % per
    from_goal = (back[:, None] == at[None, :]).astype(BF16)
    basis = jnp.dot(from_goal, basis, preferred_element_type=F32)
    return (basis[:, :width] + basis[:, width:], upper / root)


def solution(mesh):
    in_specs = (
        P("sample", None),
        P("interval", None),
        P("interval", "sample", None, None),
        P("interval", "sample"),
        P("interval", "sample"),
        P("interval", "sample"),
        P("sample"),
        P("sample"),
    )
    out_specs = (P("sample", None), P())
    return jax.shard_map(shards, mesh=mesh, in_specs=in_specs, out_specs=out_specs, check_vma=False)
```

```python
import functools
import math

import jax
import jax.numpy as jnp
from jax import lax
from jax.experimental import pallas as pl
from jax.experimental.pallas import tpu as pltpu
from jax.sharding import PartitionSpec as P

ITERS = 2
X, Z, C = 4, 8, 2
HIGH = lax.Precision.HIGHEST
F32 = jnp.float32
BF16 = jnp.bfloat16
MIB = 1024 * 1024
I16 = jnp.int16
TILE = 512
QUARTERS = 4


def block_of(x, k):
    return pl.multiple_of((k // X * X + lax.rem(x + k % X, X)) * TILE, TILE)


def node_loop(z_ref, p_ref, x, mine_ref, other_ref):
    width = mine_ref.shape[1]
    for k in range(C * X):
        z = z_ref[pl.ds(block_of(x, k), TILE), :]
        prod = jnp.dot(z, p_ref[...], preferred_element_type=F32)
        total = prod[:, :width]
        if prod.shape[1] > width:
            total = total + prod[:, width:]
        to_ref = mine_ref if k < X else other_ref
        to_ref[k % X * TILE : (k % X + 1) * TILE, :] = total


def dense_kernel(
    order_ref, node_ref, lane_ref, keep_ref, bound_ref, x_ref, blk_ref, p_ref,
    out_ref, mine_ref, other_ref, held, z, sem,
):
    nodes, rows = z.shape
    nbk, sb = held.shape[1:]
    tile = 128
    copy = pltpu.make_async_copy(blk_ref, held, sem.at[0])
    copy.start()

    def zero(i, carry):
        z[pl.ds(pl.multiple_of(i * tile, tile), tile), :] = jnp.zeros((tile, rows), BF16)
        return carry

    lax.fori_loop(0, nodes // tile, zero, 0)
    copy.wait()

    def add(i, total):
        total = jnp.where(keep_ref[i] == 1, total, 0.0) + held[order_ref[i]].astype(F32)
        node = pl.multiple_of(node_ref[i], nbk)
        lane = pl.multiple_of(lane_ref[i], sb)
        z[pl.ds(node, nbk), pl.ds(lane, sb)] = total.astype(BF16)
        return total

    unroll = 8
    total = jnp.zeros((nbk, sb), F32)
    part = nodes // QUARTERS
    backs = []
    for q in range(QUARTERS):
        first = 0 if q == 0 else bound_ref[q - 1]
        last = bound_ref[q]
        turns = (last - first) // unroll

        def several(i, total, first=first):
            for j in range(unroll):
                total = add(first + i * unroll + j, total)
            return total

        total = lax.fori_loop(0, turns, several, total)
        total = lax.fori_loop(first + turns * unroll, last, add, total)
        at = pl.ds(q * part, part)
        backs.append(pltpu.make_async_copy(z.at[at], out_ref.at[at], sem.at[1 + q]))
        backs[-1].start()
    node_loop(z, p_ref, x_ref[0], mine_ref, other_ref)
    for back in backs:
        back.wait()


def dense(blocks, row_at, col_at, count, probe, x, nodes):
    slots, nbk, sb = blocks.shape
    rows, width = probe.shape
    nrow = rows // sb
    place = col_at * nrow + row_at
    at = jnp.arange(slots, dtype=jnp.int32)
    live = at < count[0]
    key = jnp.where(live, place * slots, nodes * rows) + at
    rank = jnp.sum((key[None, :] < key[:, None]).astype(jnp.int32), axis=1)
    earlier = (place[None, :] == place[:, None]) & (at[None, :] < at[:, None])
    keep = jnp.max(earlier.astype(jnp.int32), axis=1)
    hit = rank[None, :] == at[:, None]
    order, node, lane, keep = [
        jnp.sum(jnp.where(hit, value[None, :], 0), axis=1)
        for value in (at, col_at * nbk, row_at * sb, keep)
    ]
    ends = (jnp.arange(QUARTERS, dtype=jnp.int32) + 1) * (nodes // nbk * nrow // QUARTERS)
    bound = jnp.sum((live & (place < ends[:, None])).astype(jnp.int32), axis=1)
    return pl.pallas_call(
        dense_kernel,
        out_shape=(
            pltpu.HBM((nodes, rows), BF16),
            jax.ShapeDtypeStruct((nodes // C, width), F32),
            jax.ShapeDtypeStruct((nodes // C, width), F32),
        ),
        in_specs=[pl.BlockSpec(memory_space=pltpu.SMEM)] * 6
        + [pl.BlockSpec(memory_space=pl.ANY), pl.BlockSpec(memory_space=pltpu.VMEM)],
        out_specs=(
            pl.BlockSpec(memory_space=pl.ANY),
            pl.BlockSpec(memory_space=pltpu.VMEM),
            pl.BlockSpec(memory_space=pltpu.VMEM),
        ),
        scratch_shapes=[
            pltpu.VMEM(blocks.shape, BF16),
            pltpu.VMEM((nodes, rows), BF16),
            pltpu.SemaphoreType.DMA((1 + QUARTERS,)),
        ],
        compiler_params=pltpu.CompilerParams(vmem_limit_bytes=20 * MIB),
        name="dense",
    )(
        order,
        node,
        lane,
        keep,
        bound,
        x.reshape(1),
        pltpu.with_memory_space_constraint(blocks, pltpu.HBM),
        probe,
    )


def chol_kernel(a_ref, upper_ref, inv_ref):
    n = a_ref.shape[0]
    groups = n // 8
    block = 8
    lane = lax.broadcasted_iota(jnp.int32, (8, n), 1)
    sub = lax.broadcasted_iota(jnp.int32, (8, n), 0)
    a = [a_ref[g * 8 : g * 8 + 8, :] for g in range(groups)]
    x = [(lane == sub + g * 8).astype(F32) for g in range(groups)]

    def row(value, i):
        return jnp.broadcast_to(value[i : i + 1, :], (8, n))

    def column(value, k):
        return jnp.broadcast_to(value[:, k : k + 1], (8, n))

    for k in range(0, n, block):
        g0, s = divmod(k, 8)
        cols = [column(a[g0], k + j) for j in range(block)]
        m = [[row(cols[j], s + i) for j in range(i + 1)] for i in range(block)]
        ra = [row(a[g0], s + i) for i in range(block)]
        rx = [row(x[g0], s + i) for i in range(block)]
        low = {}
        for j in range(block):
            one = 1.0 / m[j][j]
            for i in range(j + 1, block):
                low[i, j] = m[i][j] * one
                for h in range(j + 1, i + 1):
                    m[i][h] = m[i][h] - low[i, j] * m[h][j]
                ra[i] = ra[i] - low[i, j] * ra[j]
                rx[i] = rx[i] - low[i, j] * rx[j]
            ra[j], rx[j] = ra[j] * one, rx[j] * one
        for g in range(g0, groups):
            if g > g0:
                cols = [column(a[g], k + j) for j in range(block)]
            c = list(cols)
            for j in range(block):
                for h in range(j):
                    c[j] = c[j] - c[h] * low[j, h]
            if g == g0:
                c = [jnp.where(sub > s + j, c[j], 0.0) for j in range(block)]
            for j in range(block):
                a[g] = a[g] - c[j] * ra[j]
                x[g] = x[g] - c[j] * rx[j]
    for g in range(groups):
        own = lane == sub + g * 8
        diag = jnp.sum(jnp.where(own, a[g], 0.0), axis=1, keepdims=True)
        inv_root = 1.0 / jnp.sqrt(diag)
        upper_ref[g * 8 : g * 8 + 8, :] = jnp.where(lane >= sub + g * 8, a[g] * inv_root, 0.0)
        inv_ref[g * 8 : g * 8 + 8, :] = x[g] * inv_root


def factor(gram):
    shape = jax.ShapeDtypeStruct(gram.shape, F32)
    return pl.pallas_call(
        chol_kernel,
        out_shape=(shape, shape),
        compiler_params=pltpu.CompilerParams(vmem_limit_bytes=8 * MIB),
        name="factor",
    )(gram)


def two_parts(value):
    high = value.astype(BF16)
    low = (value - high.astype(F32)).astype(BF16)
    return jnp.concatenate([high, low], axis=1)


def near_kernel(z_ref, out_ref, sem):
    copy = pltpu.make_async_copy(z_ref, out_ref, sem)
    copy.start()
    copy.wait()


def near(dense_z):
    return pl.pallas_call(
        near_kernel,
        out_shape=pltpu.VMEM(dense_z.shape, dense_z.dtype),
        in_specs=[pl.BlockSpec(memory_space=pl.ANY)],
        out_specs=pl.BlockSpec(memory_space=pltpu.VMEM),
        scratch_shapes=[pltpu.SemaphoreType.DMA],
        compiler_params=pltpu.CompilerParams(vmem_limit_bytes=MIB),
        cost_estimate=pl.CostEstimate(
            flops=0, bytes_accessed=2 * dense_z.size * 2, transcendentals=0
        ),
        name="near",
    )(pltpu.with_memory_space_constraint(dense_z, pltpu.HBM))


def node_kernel(x_ref, z_ref, *refs):
    p_refs, (mine_ref, other_ref, both) = refs[:-3], refs[-3:]
    at = 0
    for p_ref in p_refs:
        size = p_ref.shape[0]
        both[at : at + size, :] = two_parts(p_ref[...])
        at += size
    node_loop(z_ref, both, x_ref[0], mine_ref, other_ref)


def node_sums(dense_z, probes, x):
    nodes, rows = dense_z.shape
    width = probes[0].shape[1]
    half = jax.ShapeDtypeStruct((nodes // C, width), F32)
    vmem = pl.BlockSpec(memory_space=pltpu.VMEM)
    return pl.pallas_call(
        node_kernel,
        out_shape=(half, half),
        in_specs=[pl.BlockSpec(memory_space=pltpu.SMEM)] + [vmem] * (1 + len(probes)),
        out_specs=(vmem, vmem),
        scratch_shapes=[pltpu.VMEM((rows, 2 * width), BF16)],
        compiler_params=pltpu.CompilerParams(vmem_limit_bytes=8 * MIB),
        name="node_sums",
    )(x.reshape(1), pltpu.with_memory_space_constraint(dense_z, pltpu.VMEM), *probes)


def image_kernel(x_ref, z_ref, *refs, nbk):
    w_refs, (out_ref, acc) = refs[:-2], refs[-2:]
    width = out_ref.shape[1]
    for step, w_ref in enumerate(w_refs):
        if w_ref.dtype == BF16:
            w = w_ref[...].reshape(TILE, width)
        else:
            parts = []
            for piece in range(TILE // nbk):
                code = w_ref[piece].astype(jnp.int32).astype(F32)
                parts.append(code[:nbk] * jnp.exp2(code[nbk : nbk + 1] - 14.0))
            w = two_parts(jnp.concatenate(parts, axis=0))
        z = z_ref[pl.ds(block_of(x_ref[0], step), TILE), :]
        prod = lax.dot_general(w, z, (((0,), (0,)), ((), ())), preferred_element_type=F32)
        if step == 0:
            acc[...] = prod
        else:
            acc[...] += prod
    total = acc[:width, :]
    for i in range(width, acc.shape[0], width):
        total = total + acc[i : i + width, :]
    out_ref[...] = total.T


def image_part(dense_z, weights, x, nbk):
    rows = dense_z.shape[1]
    width = weights[0].shape[2]
    parts = 1 if weights[0].dtype == BF16 else 2
    return pl.pallas_call(
        functools.partial(image_kernel, nbk=nbk),
        out_shape=jax.ShapeDtypeStruct((rows, width), F32),
        in_specs=[
            pl.BlockSpec(memory_space=pltpu.SMEM),
        ]
        + [pl.BlockSpec(memory_space=pltpu.VMEM)] * (1 + len(weights)),
        out_specs=pl.BlockSpec(memory_space=pltpu.VMEM),
        scratch_shapes=[pltpu.VMEM((parts * width, rows), F32)],
        compiler_params=pltpu.CompilerParams(vmem_limit_bytes=8 * MIB),
        name="image_part",
    )(x.reshape(1), pltpu.with_memory_space_constraint(dense_z, pltpu.VMEM), *weights)


def along(axis, k):
    pairs = []
    for s in range(X * Z * C):
        x, z, c = s // (Z * C), s // C % Z, s % C
        if axis == "x":
            x = (x + k) % X
        if axis == "z":
            z = (z + k) % Z
        if axis == "c":
            c = (c + k) % C
        pairs.append((s, (x * Z + z) * C + c))
    return pairs


def from_core(value):
    return lax.ppermute(value, "sample", along("c", 1))


def exchange(value):
    groups = {}
    for device in range(X * Z * C):
        groups.setdefault((device // (Z * C), device % C), []).append(device)
    return lax.all_to_all(
        value,
        "sample",
        split_axis=0,
        concat_axis=0,
        axis_index_groups=list(groups.values()),
        tiled=True,
    )


def coded(value):
    top = jnp.max(jnp.abs(value), axis=1, keepdims=True)
    power = jnp.floor(jnp.log2(jnp.maximum(top, 1e-30))) + 1.0
    power = jnp.clip(power, -100.0, 127.0)
    return value * jnp.exp2(14.0 - power), power


def whole(value):
    return jnp.round(value).astype(I16)


def decoded(code, power):
    return code.astype(F32) * jnp.exp2(power.astype(F32) - 14.0)


def message(value, gram, lines):
    scaled, power = coded(value)
    rows = [whole(scaled), power.astype(I16)]
    if gram is not None:
        scaled, power = coded(gram)
        high = jnp.round(scaled)
        rows += [high.astype(I16), whole((scaled - high) * 2.0**14), power.astype(I16)]
    rows = jnp.concatenate(rows, axis=1)
    return jnp.pad(rows, ((0, 0), (0, lines - rows.shape[1]), (0, 0)))


def read_value(rows, own):
    return decoded(rows[:, :own], rows[:, own : own + 1])


def read_gram(rows, own, lines):
    at = own + 1
    code = rows[:, at : at + lines].astype(F32)
    code = code + rows[:, at + lines : at + 2 * lines].astype(F32) * 2.0**-14
    return decoded(code, rows[:, at + 2 * lines : at + 2 * lines + 1])


def sum_nodes(mine, gram, others):
    width = mine.shape[1]
    lines = width // (X * Z * C)
    mine = mine.reshape(X, -1, width)
    rows = mine.shape[1]
    extra = None if gram is None else gram.reshape(X, -1, width)
    size = rows + 8 if gram is None else rows + 8 + 2 * Z * lines
    sent = message(mine[1:], None if gram is None else extra[1:], size)
    got = [lax.ppermute(sent[k - 1], "sample", along("x", k)) for k in range(1, X)]
    total = mine[0] + sum(read_value(part[None], rows)[0] for part in got)
    if gram is not None:
        gram = extra[0] + sum(read_gram(part[None], rows, Z * lines)[0] for part in got)
        gram = gram.reshape(Z, lines, width)
    sent = message(total.reshape(Z, -1, width), gram, rows // Z + 8)
    sent, others = lax.optimization_barrier((sent, others))
    got = exchange(sent.reshape(-1, width))
    got, others = lax.optimization_barrier((got, others))
    got = got.reshape(Z, -1, width)
    if gram is not None:
        gram = jnp.sum(read_gram(got, rows // Z, lines), axis=0)
    return jnp.sum(read_value(got, rows // Z), axis=0), gram, others


def spread(own, dense_z, others):
    copies = jnp.broadcast_to(own[None], (Z,) + own.shape).reshape(-1, own.shape[1])
    copies, others = lax.optimization_barrier((copies, others))
    got = exchange(copies)
    got, dense_z, others = lax.optimization_barrier((got, dense_z, others))
    got = got.reshape((Z,) + own.shape)
    mine = [lax.ppermute(got, "sample", along("x", -k)) for k in range(1, X)]
    mine, near_z = lax.optimization_barrier((mine, near(dense_z)))
    mine = [got] + mine
    return mine + [from_core(part) for part in mine], near_z, others


def scatter_interval(value, ny):
    piece = value.shape[0] // ny
    total = value[:piece]
    for k in range(1, ny):
        sent = value[k * piece : (k + 1) * piece]
        total = total + lax.ppermute(sent, "interval", [(i, (i + k) % ny) for i in range(ny)])
    return total


def gather_interval(value, ny):
    parts = [value]
    for k in range(1, ny):
        parts.append(lax.ppermute(value, "interval", [(i, (i - k) % ny) for i in range(ny)]))
    return parts


def split(value, count):
    parts = []
    for _ in range(count):
        part = lax.reduce_precision(value, exponent_bits=8, mantissa_bits=7)
        value = value - part
        parts.append(part.astype(BF16))
    return jnp.concatenate(parts, axis=1)


def gram_of(image):
    return lax.dot_general(
        image, image, (((0,), (0,)), ((), ())), precision=HIGH, preferred_element_type=F32
    )


def shards(
    probes, lengths, incidence, block_rows, block_cols, block_count, tree_sample, tree_position
):
    ndev = lax.axis_size("sample")
    ny = lax.axis_size("interval")
    mine = lax.axis_index("sample")
    iy = lax.axis_index("interval")
    rows_here, width = probes.shape
    samples = rows_here * ndev
    root = math.sqrt(samples)
    share = rows_here // ndev
    quarter = rows_here // ny
    blocks = incidence[0]
    slots, nbk, sb = blocks.shape
    nodes = ndev * nbk
    nrow = rows_here // sb
    turn = nrow // ny

    at = jnp.arange(rows_here, dtype=jnp.int32)
    rank = jnp.sum((tree_position[None, :] < tree_position[:, None]).astype(jnp.int32), axis=1)
    to_send = (at[:, None] == rank[None, :]).astype(BF16)
    sent = jnp.dot(to_send, probes, preferred_element_type=F32).astype(BF16)
    moved = lax.all_to_all(sent, "sample", split_axis=0, concat_axis=0, tiled=True)

    source = tree_sample // rows_here
    same = (source[None, :] == source[:, None]) & (at[None, :] < at[:, None])
    order = jnp.sum(same.astype(jnp.int32), axis=1)
    source = jnp.roll(source, -iy * quarter)
    order = jnp.roll(order, -iy * quarter)
    slot = source * share + order
    rows = block_rows[0]
    cols = block_cols[0]
    row_at = (rows + nrow - iy * turn) % nrow
    col_at = ((cols + mine) % C) * (ndev // C) + cols // C
    own_lens = lax.dynamic_slice_in_dim(lengths[0], mine * nbk, nbk, 0)

    def scale(owned):
        return own_lens[:, None] * owned / samples

    core = mine % C
    here = mine // (Z * C)
    from_moved = (slot[:, None] == at[None, :]).astype(BF16)
    tree_probe = jnp.dot(from_moved, moved, preferred_element_type=F32).astype(BF16)
    dense_z, first, second = dense(
        blocks, row_at, col_at, block_count[0], tree_probe, here, nodes
    )
    tied = (own_lens, rank, source, order, core, here)
    owned, _, tied = sum_nodes(first + from_core(second), None, tied)
    own_lens = tied[0]
    weights, near_z, tied = spread(scale(owned).astype(BF16), dense_z, tied)
    own_lens, core, here = tied[0], tied[4], tied[5]
    part = image_part(near_z, weights, here, nbk)
    piece, far_z = lax.optimization_barrier((scatter_interval(part, ny), dense_z))
    pieces = gather_interval(piece, ny)

    first, second = node_sums(near(far_z), pieces, here)
    first, second, pieces = lax.optimization_barrier((first, second, pieces))
    second = from_core(second)
    gram = jnp.split(gram_of(jnp.concatenate(pieces, axis=0)), C, axis=0)
    gram = [jnp.where(core == c, gram[0], gram[1]) for c in range(C)]
    gram = gram[0] + from_core(gram[1])
    lines = width // ndev
    gram = jnp.roll(gram, -here * (Z * lines), axis=0)
    owned, gram, tied = sum_nodes(first + second, gram, tied)
    own_lens = tied[0]
    sent = message(scale(owned)[None], gram[None], nbk + 16)[0]
    weights, near_z, tied = spread(sent, dense_z, tied)
    rank, source, order, core, here = tied[1:]
    part = image_part(near_z, weights, here, nbk)
    part, weights, here, core = lax.optimization_barrier((part, weights, here, core))
    gram = [read_gram(got, nbk, lines).reshape(-1, width) for got in weights]
    gram = [jnp.concatenate(gram[c * X : (c + 1) * X], axis=0) for c in range(C)]
    gram = [jnp.roll(half, here * (Z * lines), axis=0) for half in gram]
    gram = jnp.concatenate([jnp.where(core == c, gram[0], gram[1]) for c in range(C)], axis=0)
    _, inverse = factor(gram)

    per = share // ny
    jrel = (order // per + ny - iy) % ny
    goal = jrel * quarter + source * per + order % per
    to_goal = (at[:, None] == goal[None, :]).astype(BF16)
    pieces = jnp.dot(to_goal, split(part, 3), preferred_element_type=F32)
    part = pieces[:, :width] + pieces[:, width : 2 * width] + pieces[:, 2 * width :]
    image = scatter_interval(part, ny)
    image = root * jnp.dot(image, inverse.T, precision=HIGH, preferred_element_type=F32)
    gram = gram_of(image).reshape(ndev, -1, width)
    image = jnp.concatenate([image.reshape(ndev, per, width), gram], axis=1)
    image = jnp.pad(image, ((0, 0), (0, -image.shape[1] % 8), (0, 0)))
    image, rank = lax.optimization_barrier((image, rank))
    image = lax.all_to_all(
        image.reshape(-1, width), "sample", split_axis=0, concat_axis=0, tiled=True
    )
    image, rank = lax.optimization_barrier((image, rank))
    image = image.reshape(ndev, -1, width)
    gram = jnp.sum(image[:, per : per + lines], axis=0)
    image = image[:, :per].reshape(quarter, width)
    image = gather_interval(jnp.concatenate([image, gram, jnp.zeros((-lines % 8, width), F32)], axis=0), ny)
    image = jnp.stack(image)
    gram = jnp.sum(image[:, quarter : quarter + lines], axis=0)
    image = image[:, :quarter].reshape(rows_here, width)
    k = rank % share
    back = ((k // per + ny - iy) % ny) * quarter + (rank // share) * per + k % per
    from_goal = (back[:, None] == at[None, :]).astype(BF16)
    pieces = jnp.dot(from_goal, split(image, 3), preferred_element_type=F32)
    image = pieces[:, :width] + pieces[:, width : 2 * width] + pieces[:, 2 * width :]
    gram = jnp.broadcast_to(gram[None], (ndev,) + gram.shape).reshape(-1, width)
    gram, image = lax.optimization_barrier((gram, image))
    gram = lax.all_to_all(gram, "sample", split_axis=0, concat_axis=0, tiled=True)
    gram, image = lax.optimization_barrier((gram, image))
    upper, inverse = factor(gram)
    basis = root * jnp.dot(image, inverse.T, precision=HIGH, preferred_element_type=F32)
    return (basis, upper / root)


def solution(mesh):
    in_specs = (
        P("sample", None),
        P("interval", None),
        P("interval", "sample", None, None),
        P("interval", "sample"),
        P("interval", "sample"),
        P("interval", "sample"),
        P("sample"),
        P("sample"),
    )
    out_specs = (P("sample", None), P())
    return jax.shard_map(shards, mesh=mesh, in_specs=in_specs, out_specs=out_specs, check_vma=False)
```

```python
import functools
import math

import jax
import jax.numpy as jnp
from jax import lax
from jax.experimental import pallas as pl
from jax.experimental.pallas import tpu as pltpu
from jax.sharding import PartitionSpec as P

ITERS = 2
X, Z, C = 4, 8, 2
HIGH = lax.Precision.HIGHEST
F32 = jnp.float32
BF16 = jnp.bfloat16
MIB = 1024 * 1024
I16 = jnp.int16
TILE = 512
QUARTERS = 4


def block_of(x, k):
    return pl.multiple_of((k // X * X + lax.rem(x + k % X, X)) * TILE, TILE)


def node_loop(z_ref, p_ref, x, mine_ref, other_ref):
    width = mine_ref.shape[1]
    for k in range(C * X):
        z = z_ref[pl.ds(block_of(x, k), TILE), :]
        prod = jnp.dot(z, p_ref[...], preferred_element_type=F32)
        total = prod[:, :width]
        if prod.shape[1] > width:
            total = total + prod[:, width:]
        to_ref = mine_ref if k < X else other_ref
        to_ref[k % X * TILE : (k % X + 1) * TILE, :] = total


def dense_kernel(
    order_ref, node_ref, lane_ref, keep_ref, bound_ref, x_ref, blk_ref, p_ref,
    out_ref, mine_ref, other_ref, held, z, sem,
):
    nodes, rows = z.shape
    nbk, sb = held.shape[1:]
    tile = 128
    copy = pltpu.make_async_copy(blk_ref, held, sem.at[0])
    copy.start()

    def zero(i, carry):
        z[pl.ds(pl.multiple_of(i * tile, tile), tile), :] = jnp.zeros((tile, rows), BF16)
        return carry

    lax.fori_loop(0, nodes // tile, zero, 0)
    copy.wait()

    def add(i, total):
        total = jnp.where(keep_ref[i] == 1, total, 0.0) + held[order_ref[i]].astype(F32)
        node = pl.multiple_of(node_ref[i], nbk)
        lane = pl.multiple_of(lane_ref[i], sb)
        z[pl.ds(node, nbk), pl.ds(lane, sb)] = total.astype(BF16)
        return total

    unroll = 8
    total = jnp.zeros((nbk, sb), F32)
    part = nodes // QUARTERS
    backs = []
    for q in range(QUARTERS):
        first = 0 if q == 0 else bound_ref[q - 1]
        last = bound_ref[q]
        turns = (last - first) // unroll

        def several(i, total, first=first):
            for j in range(unroll):
                total = add(first + i * unroll + j, total)
            return total

        total = lax.fori_loop(0, turns, several, total)
        total = lax.fori_loop(first + turns * unroll, last, add, total)
        at = pl.ds(q * part, part)
        backs.append(pltpu.make_async_copy(z.at[at], out_ref.at[at], sem.at[1 + q]))
        backs[-1].start()
    node_loop(z, p_ref, x_ref[0], mine_ref, other_ref)
    for back in backs:
        back.wait()


def dense(blocks, row_at, col_at, count, probe, x, nodes):
    slots, nbk, sb = blocks.shape
    rows, width = probe.shape
    nrow = rows // sb
    place = col_at * nrow + row_at
    at = jnp.arange(slots, dtype=jnp.int32)
    live = at < count[0]
    key = jnp.where(live, place * slots, nodes * rows) + at
    rank = jnp.sum((key[None, :] < key[:, None]).astype(jnp.int32), axis=1)
    earlier = (place[None, :] == place[:, None]) & (at[None, :] < at[:, None])
    keep = jnp.max(earlier.astype(jnp.int32), axis=1)
    hit = rank[None, :] == at[:, None]
    order, node, lane, keep = [
        jnp.sum(jnp.where(hit, value[None, :], 0), axis=1)
        for value in (at, col_at * nbk, row_at * sb, keep)
    ]
    ends = (jnp.arange(QUARTERS, dtype=jnp.int32) + 1) * (nodes // nbk * nrow // QUARTERS)
    bound = jnp.sum((live & (place < ends[:, None])).astype(jnp.int32), axis=1)
    return pl.pallas_call(
        dense_kernel,
        out_shape=(
            pltpu.HBM((nodes, rows), BF16),
            jax.ShapeDtypeStruct((nodes // C, width), F32),
            jax.ShapeDtypeStruct((nodes // C, width), F32),
        ),
        in_specs=[pl.BlockSpec(memory_space=pltpu.SMEM)] * 6
        + [pl.BlockSpec(memory_space=pl.ANY), pl.BlockSpec(memory_space=pltpu.VMEM)],
        out_specs=(
            pl.BlockSpec(memory_space=pl.ANY),
            pl.BlockSpec(memory_space=pltpu.VMEM),
            pl.BlockSpec(memory_space=pltpu.VMEM),
        ),
        scratch_shapes=[
            pltpu.VMEM(blocks.shape, BF16),
            pltpu.VMEM((nodes, rows), BF16),
            pltpu.SemaphoreType.DMA((1 + QUARTERS,)),
        ],
        compiler_params=pltpu.CompilerParams(vmem_limit_bytes=20 * MIB),
        name="dense",
    )(
        order,
        node,
        lane,
        keep,
        bound,
        x.reshape(1),
        pltpu.with_memory_space_constraint(blocks, pltpu.HBM),
        probe,
    )


def chol_kernel(a_ref, upper_ref, inv_ref, *, root):
    n = a_ref.shape[0]
    groups = n // 8
    block = 8
    lane = lax.broadcasted_iota(jnp.int32, (8, n), 1)
    sub = lax.broadcasted_iota(jnp.int32, (8, n), 0)
    a = [a_ref[g * 8 : g * 8 + 8, :] for g in range(groups)]
    x = [(lane == sub + g * 8).astype(F32) for g in range(groups)]

    def row(value, i):
        return jnp.broadcast_to(value[i : i + 1, :], (8, n))

    def column(value, k):
        return jnp.broadcast_to(value[:, k : k + 1], (8, n))

    for k in range(0, n, block):
        g0, s = divmod(k, 8)
        cols = [column(a[g0], k + j) for j in range(block)]
        m = [[row(cols[j], s + i) for j in range(i + 1)] for i in range(block)]
        ra = [row(a[g0], s + i) for i in range(block)]
        rx = [row(x[g0], s + i) for i in range(block)]
        low = {}
        for j in range(block):
            one = 1.0 / m[j][j]
            for i in range(j + 1, block):
                low[i, j] = m[i][j] * one
                for h in range(j + 1, i + 1):
                    m[i][h] = m[i][h] - low[i, j] * m[h][j]
                ra[i] = ra[i] - low[i, j] * ra[j]
                rx[i] = rx[i] - low[i, j] * rx[j]
            ra[j], rx[j] = ra[j] * one, rx[j] * one
        for g in range(g0, groups):
            if g > g0:
                cols = [column(a[g], k + j) for j in range(block)]
            c = list(cols)
            for j in range(block):
                for h in range(j):
                    c[j] = c[j] - c[h] * low[j, h]
            if g == g0:
                c = [jnp.where(sub > s + j, c[j], 0.0) for j in range(block)]
            for j in range(block):
                a[g] = a[g] - c[j] * ra[j]
                x[g] = x[g] - c[j] * rx[j]
    for g in range(groups):
        own = lane == sub + g * 8
        diag = jnp.sum(jnp.where(own, a[g], 0.0), axis=1, keepdims=True)
        inv_root = 1.0 / jnp.sqrt(diag)
        upper_ref[g * 8 : g * 8 + 8, :] = jnp.where(
            lane >= sub + g * 8, a[g] * (inv_root / root), 0.0
        )
        inv_ref[g * 8 : g * 8 + 8, :] = x[g] * inv_root


def factor(gram, root):
    shape = jax.ShapeDtypeStruct(gram.shape, F32)
    return pl.pallas_call(
        functools.partial(chol_kernel, root=root),
        out_shape=(shape, shape),
        compiler_params=pltpu.CompilerParams(vmem_limit_bytes=8 * MIB),
        name="factor",
    )(gram)


def two_parts(value):
    high = value.astype(BF16)
    low = (value - high.astype(F32)).astype(BF16)
    return jnp.concatenate([high, low], axis=1)


def near_kernel(z_ref, out_ref, sem):
    copy = pltpu.make_async_copy(z_ref, out_ref, sem)
    copy.start()
    copy.wait()


def near(dense_z):
    return pl.pallas_call(
        near_kernel,
        out_shape=pltpu.VMEM(dense_z.shape, dense_z.dtype),
        in_specs=[pl.BlockSpec(memory_space=pl.ANY)],
        out_specs=pl.BlockSpec(memory_space=pltpu.VMEM),
        scratch_shapes=[pltpu.SemaphoreType.DMA],
        compiler_params=pltpu.CompilerParams(vmem_limit_bytes=MIB),
        cost_estimate=pl.CostEstimate(
            flops=0, bytes_accessed=2 * dense_z.size * 2, transcendentals=0
        ),
        name="near",
    )(pltpu.with_memory_space_constraint(dense_z, pltpu.HBM))


def node_kernel(x_ref, z_ref, *refs):
    c_refs, (mine_ref, other_ref, image_ref, both) = refs[:-4], refs[-4:]
    count = len(c_refs)
    size = image_ref.shape[0] // count
    for m in range(count):
        total = None
        for k, c_ref in enumerate(c_refs):
            code = c_ref[(m - k) % count].astype(jnp.int32).astype(F32)
            term = code[:size] * jnp.exp2(code[size : size + 1] - 14.0)
            total = term if total is None else total + term
        at = slice(m * size, (m + 1) * size)
        image_ref[at, :] = total
        both[at, :] = two_parts(total)
    node_loop(z_ref, both, x_ref[0], mine_ref, other_ref)


def node_sums(dense_z, codes, x):
    nodes, rows = dense_z.shape
    width = codes[0].shape[-1]
    half = jax.ShapeDtypeStruct((nodes // C, width), F32)
    vmem = pl.BlockSpec(memory_space=pltpu.VMEM)
    return pl.pallas_call(
        node_kernel,
        out_shape=(half, half, jax.ShapeDtypeStruct((rows, width), F32)),
        in_specs=[pl.BlockSpec(memory_space=pltpu.SMEM)] + [vmem] * (1 + len(codes)),
        out_specs=(vmem, vmem, vmem),
        scratch_shapes=[pltpu.VMEM((rows, 2 * width), BF16)],
        compiler_params=pltpu.CompilerParams(vmem_limit_bytes=8 * MIB),
        name="node_sums",
    )(x.reshape(1), pltpu.with_memory_space_constraint(dense_z, pltpu.VMEM), *codes)


def image_kernel(x_ref, z_ref, *refs, nbk):
    w_refs, (out_ref, acc) = refs[:-2], refs[-2:]
    width = out_ref.shape[1]
    for step, w_ref in enumerate(w_refs):
        if w_ref.dtype == BF16:
            w = w_ref[...].reshape(TILE, width)
        else:
            parts = []
            for piece in range(TILE // nbk):
                code = w_ref[piece].astype(jnp.int32).astype(F32)
                parts.append(code[:nbk] * jnp.exp2(code[nbk : nbk + 1] - 14.0))
            w = two_parts(jnp.concatenate(parts, axis=0))
        z = z_ref[pl.ds(block_of(x_ref[0], step), TILE), :]
        prod = lax.dot_general(w, z, (((0,), (0,)), ((), ())), preferred_element_type=F32)
        if step == 0:
            acc[...] = prod
        else:
            acc[...] += prod
    total = acc[:width, :]
    for i in range(width, acc.shape[0], width):
        total = total + acc[i : i + width, :]
    out_ref[...] = total.T


def image_part(dense_z, weights, x, nbk):
    rows = dense_z.shape[1]
    width = weights[0].shape[2]
    parts = 1 if weights[0].dtype == BF16 else 2
    return pl.pallas_call(
        functools.partial(image_kernel, nbk=nbk),
        out_shape=jax.ShapeDtypeStruct((rows, width), F32),
        in_specs=[
            pl.BlockSpec(memory_space=pltpu.SMEM),
        ]
        + [pl.BlockSpec(memory_space=pltpu.VMEM)] * (1 + len(weights)),
        out_specs=pl.BlockSpec(memory_space=pltpu.VMEM),
        scratch_shapes=[pltpu.VMEM((parts * width, rows), F32)],
        compiler_params=pltpu.CompilerParams(vmem_limit_bytes=8 * MIB),
        name="image_part",
    )(x.reshape(1), pltpu.with_memory_space_constraint(dense_z, pltpu.VMEM), *weights)


def along(axis, k):
    pairs = []
    for s in range(X * Z * C):
        x, z, c = s // (Z * C), s // C % Z, s % C
        if axis == "x":
            x = (x + k) % X
        if axis == "z":
            z = (z + k) % Z
        if axis == "c":
            c = (c + k) % C
        pairs.append((s, (x * Z + z) * C + c))
    return pairs


def from_core(value):
    return lax.ppermute(value, "sample", along("c", 1))


def exchange(value):
    groups = {}
    for device in range(X * Z * C):
        groups.setdefault((device // (Z * C), device % C), []).append(device)
    return lax.all_to_all(
        value,
        "sample",
        split_axis=0,
        concat_axis=0,
        axis_index_groups=list(groups.values()),
        tiled=True,
    )


def coded(value):
    top = jnp.max(jnp.abs(value), axis=1, keepdims=True)
    power = jnp.floor(jnp.log2(jnp.maximum(top, 1e-30))) + 1.0
    power = jnp.clip(power, -100.0, 127.0)
    return value * jnp.exp2(14.0 - power), power


def whole(value):
    return jnp.round(value).astype(I16)


def decoded(code, power):
    return code.astype(F32) * jnp.exp2(power.astype(F32) - 14.0)


def message(value, gram, multiple=8):
    scaled, power = coded(value)
    rows = [whole(scaled), power.astype(I16)]
    if gram is not None:
        scaled, power = coded(gram)
        high = jnp.round(scaled)
        rows += [high.astype(I16), whole((scaled - high) * 2.0**14), power.astype(I16)]
    rows = jnp.concatenate(rows, axis=1)
    return jnp.pad(rows, ((0, 0), (0, -rows.shape[1] % multiple), (0, 0)))


def read_value(rows, own):
    return decoded(rows[:, :own], rows[:, own : own + 1])


def read_gram(rows, own, lines):
    at = own + 1
    code = rows[:, at : at + lines].astype(F32)
    code = code + rows[:, at + lines : at + 2 * lines].astype(F32) * 2.0**-14
    return decoded(code, rows[:, at + 2 * lines : at + 2 * lines + 1])


def sum_nodes(mine, gram, others):
    width = mine.shape[1]
    lines = width // (X * Z)
    mine = mine.reshape(X, -1, width)
    rows = mine.shape[1]
    extra = None if gram is None else gram.reshape(X, -1, width)
    sent = message(mine[1:], None if gram is None else extra[1:])
    got = [lax.ppermute(sent[k - 1], "sample", along("x", k)) for k in range(1, X)]
    total = mine[0] + sum(read_value(part[None], rows)[0] for part in got)
    if gram is not None:
        gram = extra[0] + sum(read_gram(part[None], rows, Z * lines)[0] for part in got)
        gram = gram.reshape(Z, lines, width)
    sent = message(total.reshape(Z, -1, width), gram)
    sent, others = lax.optimization_barrier((sent, others))
    got = exchange(sent.reshape(-1, width))
    got, others = lax.optimization_barrier((got, others))
    got = got.reshape(Z, -1, width)
    if gram is not None:
        gram = jnp.sum(read_gram(got, rows // Z, lines), axis=0)
    return jnp.sum(read_value(got, rows // Z), axis=0), gram, others


def spread(own, dense_z, others):
    copies = jnp.broadcast_to(own[None], (Z,) + own.shape).reshape(-1, own.shape[1])
    copies, others = lax.optimization_barrier((copies, others))
    got = exchange(copies)
    got, dense_z, others = lax.optimization_barrier((got, dense_z, others))
    got = got.reshape((Z,) + own.shape)
    mine = [lax.ppermute(got, "sample", along("x", -k)) for k in range(1, X)]
    mine, near_z = lax.optimization_barrier((mine, near(dense_z)))
    mine = [got] + mine
    return mine + [from_core(part) for part in mine], near_z, others


def scatter_interval(value, ny):
    piece = value.shape[0] // ny
    total = value[:piece]
    for k in range(1, ny):
        sent = value[k * piece : (k + 1) * piece]
        total = total + lax.ppermute(sent, "interval", [(i, (i + k) % ny) for i in range(ny)])
    return total


def gather_interval(value, ny):
    parts = [value]
    for k in range(1, ny):
        parts.append(lax.ppermute(value, "interval", [(i, (i - k) % ny) for i in range(ny)]))
    return parts


def split(value, count):
    parts = []
    for _ in range(count):
        part = lax.reduce_precision(value, exponent_bits=8, mantissa_bits=7)
        value = value - part
        parts.append(part.astype(BF16))
    return jnp.concatenate(parts, axis=1)


def gram_of(image):
    return lax.dot_general(
        image, image, (((0,), (0,)), ((), ())), precision=HIGH, preferred_element_type=F32
    )


def shards(
    probes, lengths, incidence, block_rows, block_cols, block_count, tree_sample, tree_position
):
    ndev = lax.axis_size("sample")
    ny = lax.axis_size("interval")
    mine = lax.axis_index("sample")
    iy = lax.axis_index("interval")
    rows_here, width = probes.shape
    samples = rows_here * ndev
    root = math.sqrt(samples)
    share = rows_here // ndev
    quarter = rows_here // ny
    blocks = incidence[0]
    slots, nbk, sb = blocks.shape
    nodes = ndev * nbk
    nrow = rows_here // sb
    turn = nrow // ny

    at = jnp.arange(rows_here, dtype=jnp.int32)
    rank = jnp.sum((tree_position[None, :] < tree_position[:, None]).astype(jnp.int32), axis=1)
    to_send = (at[:, None] == rank[None, :]).astype(BF16)
    sent = jnp.dot(to_send, probes, preferred_element_type=F32).astype(BF16)
    moved = lax.all_to_all(sent, "sample", split_axis=0, concat_axis=0, tiled=True)

    source = tree_sample // rows_here
    same = (source[None, :] == source[:, None]) & (at[None, :] < at[:, None])
    order = jnp.sum(same.astype(jnp.int32), axis=1)
    source = jnp.roll(source, -iy * quarter)
    order = jnp.roll(order, -iy * quarter)
    slot = source * share + order
    rows = block_rows[0]
    cols = block_cols[0]
    row_at = (rows + nrow - iy * turn) % nrow
    col_at = ((cols + mine) % C) * (ndev // C) + cols // C
    own_lens = lax.dynamic_slice_in_dim(lengths[0], mine * nbk, nbk, 0)

    def scale(owned):
        return own_lens[:, None] * owned / samples

    here = mine // (Z * C)
    col_at, own_lens = lax.optimization_barrier((col_at, own_lens))
    from_moved = (slot[:, None] == at[None, :]).astype(BF16)
    tree_probe = jnp.dot(from_moved, moved, preferred_element_type=F32).astype(BF16)
    dense_z, first, second = dense(
        blocks, row_at, col_at, block_count[0], tree_probe, here, nodes
    )
    tied = (own_lens, rank, source, order, here)
    owned, _, tied = sum_nodes(first + from_core(second), None, tied)
    own_lens = tied[0]
    weights, near_z, tied = spread(scale(owned).astype(BF16), dense_z, tied)
    own_lens, here = tied[0], tied[4]
    part = image_part(near_z, weights, here, nbk)
    code = message(part.reshape(ny, quarter, width), None, 16)
    code, far_z = lax.optimization_barrier((code, dense_z))
    codes = gather_interval(code, ny)

    first, second, image = node_sums(near(far_z), codes, here)
    second = from_core(second)
    gram = gram_of(image)
    lines = width // (X * Z)
    gram = jnp.roll(gram, -here * (Z * lines), axis=0)
    owned, gram, tied = sum_nodes(first + second, gram, tied)
    own_lens = tied[0]
    sent = message(scale(owned)[None], gram[None], 16)[0]
    weights, near_z, tied = spread(sent, dense_z, tied)
    rank, source, order, here = tied[1:]
    part = image_part(near_z, weights, here, nbk)
    part, weights, here = lax.optimization_barrier((part, weights, here))
    gram = [read_gram(got, nbk, lines).reshape(-1, width) for got in weights]
    gram = jnp.concatenate([gram[k] + gram[X + k] for k in range(X)], axis=0)
    gram = jnp.roll(gram, here * (Z * lines), axis=0)
    lines = width // ndev
    _, inverse = factor(gram, root)

    per = share // ny
    jrel = (order // per + ny - iy) % ny
    goal = jrel * quarter + source * per + order % per
    to_goal = (at[:, None] == goal[None, :]).astype(BF16)
    pieces = jnp.dot(to_goal, split(part, 3), preferred_element_type=F32)
    part = pieces[:, :width] + pieces[:, width : 2 * width] + pieces[:, 2 * width :]
    image = scatter_interval(part, ny)
    image = root * jnp.dot(image, inverse.T, precision=HIGH, preferred_element_type=F32)
    gram = gram_of(image).reshape(ndev, -1, width)
    image = jnp.concatenate([image.reshape(ndev, per, width), gram], axis=1)
    image = jnp.pad(image, ((0, 0), (0, -image.shape[1] % 8), (0, 0)))
    image, rank, iy = lax.optimization_barrier((image, rank, iy))
    image = lax.all_to_all(
        image.reshape(-1, width), "sample", split_axis=0, concat_axis=0, tiled=True
    )
    image, rank, iy = lax.optimization_barrier((image, rank, iy))
    image = image.reshape(ndev, -1, width)
    gram = jnp.sum(image[:, per : per + lines], axis=0)
    image = image[:, :per].reshape(quarter, width)
    image = gather_interval(jnp.concatenate([image, gram, jnp.zeros((-lines % 8, width), F32)], axis=0), ny)
    image = jnp.stack(image)
    gram = jnp.sum(image[:, quarter : quarter + lines], axis=0)
    image = image[:, :quarter].reshape(rows_here, width)
    k = rank % share
    back = ((k // per + ny - iy) % ny) * quarter + (rank // share) * per + k % per
    from_goal = (back[:, None] == at[None, :]).astype(BF16)
    pieces = jnp.dot(from_goal, split(image, 3), preferred_element_type=F32)
    image = pieces[:, :width] + pieces[:, width : 2 * width] + pieces[:, 2 * width :]
    gram = jnp.broadcast_to(gram[None], (ndev,) + gram.shape).reshape(-1, width)
    gram, image = lax.optimization_barrier((gram, image))
    gram = lax.all_to_all(gram, "sample", split_axis=0, concat_axis=0, tiled=True)
    gram, image = lax.optimization_barrier((gram, image))
    upper, inverse = factor(gram, root)
    basis = root * jnp.dot(image, inverse.T, precision=HIGH, preferred_element_type=F32)
    return (basis, upper)


def solution(mesh):
    in_specs = (
        P("sample", None),
        P("interval", None),
        P("interval", "sample", None, None),
        P("interval", "sample"),
        P("interval", "sample"),
        P("interval", "sample"),
        P("sample"),
        P("sample"),
    )
    out_specs = (P("sample", None), P())
    return jax.shard_map(shards, mesh=mesh, in_specs=in_specs, out_specs=out_specs, check_vma=False)
```

```python
import functools
import math

import jax
import jax.numpy as jnp
from jax import lax
from jax.experimental import pallas as pl
from jax.experimental.pallas import tpu as pltpu
from jax.sharding import PartitionSpec as P

ITERS = 2
X, Z, C = 4, 8, 2
HIGH = lax.Precision.HIGHEST
F32 = jnp.float32
BF16 = jnp.bfloat16
MIB = 1024 * 1024
I16 = jnp.int16
TILE = 512
QUARTERS = 4


def block_of(x, k):
    return pl.multiple_of((k // X * X + lax.rem(x + k % X, X)) * TILE, TILE)


def node_loop(z_ref, p_ref, x, mine_ref, other_ref):
    width = mine_ref.shape[1]
    for k in range(C * X):
        z = z_ref[pl.ds(block_of(x, k), TILE), :]
        prod = jnp.dot(z, p_ref[...], preferred_element_type=F32)
        total = prod[:, :width]
        if prod.shape[1] > width:
            total = total + prod[:, width:]
        to_ref = mine_ref if k < X else other_ref
        to_ref[k % X * TILE : (k % X + 1) * TILE, :] = total


def dense_kernel(
    order_ref, node_ref, lane_ref, keep_ref, bound_ref, x_ref, blk_ref, p_ref,
    out_ref, mine_ref, other_ref, held, z, sem,
):
    nodes, rows = z.shape
    nbk, sb = held.shape[1:]
    tile = 128
    copy = pltpu.make_async_copy(blk_ref, held, sem.at[0])
    copy.start()

    def zero(i, carry):
        z[pl.ds(pl.multiple_of(i * tile, tile), tile), :] = jnp.zeros((tile, rows), BF16)
        return carry

    lax.fori_loop(0, nodes // tile, zero, 0)
    copy.wait()

    def add(i, total):
        total = jnp.where(keep_ref[i] == 1, total, 0.0) + held[order_ref[i]].astype(F32)
        node = pl.multiple_of(node_ref[i], nbk)
        lane = pl.multiple_of(lane_ref[i], sb)
        z[pl.ds(node, nbk), pl.ds(lane, sb)] = total.astype(BF16)
        return total

    unroll = 8
    total = jnp.zeros((nbk, sb), F32)
    part = nodes // QUARTERS
    backs = []
    for q in range(QUARTERS):
        first = 0 if q == 0 else bound_ref[q - 1]
        last = bound_ref[q]
        turns = (last - first) // unroll

        def several(i, total, first=first):
            for j in range(unroll):
                total = add(first + i * unroll + j, total)
            return total

        total = lax.fori_loop(0, turns, several, total)
        total = lax.fori_loop(first + turns * unroll, last, add, total)
        at = pl.ds(q * part, part)
        backs.append(pltpu.make_async_copy(z.at[at], out_ref.at[at], sem.at[1 + q]))
        backs[-1].start()
    node_loop(z, p_ref, x_ref[0], mine_ref, other_ref)
    for back in backs:
        back.wait()


def dense(blocks, row_at, col_at, count, probe, x, nodes):
    slots, nbk, sb = blocks.shape
    rows, width = probe.shape
    nrow = rows // sb
    place = col_at * nrow + row_at
    at = jnp.arange(slots, dtype=jnp.int32)
    live = at < count[0]
    key = jnp.where(live, place * slots, nodes * rows) + at
    rank = jnp.sum((key[None, :] < key[:, None]).astype(jnp.int32), axis=1)
    earlier = (place[None, :] == place[:, None]) & (at[None, :] < at[:, None])
    keep = jnp.max(earlier.astype(jnp.int32), axis=1)
    hit = rank[None, :] == at[:, None]
    order, node, lane, keep = [
        jnp.sum(jnp.where(hit, value[None, :], 0), axis=1)
        for value in (at, col_at * nbk, row_at * sb, keep)
    ]
    ends = (jnp.arange(QUARTERS, dtype=jnp.int32) + 1) * (nodes // nbk * nrow // QUARTERS)
    bound = jnp.sum((live & (place < ends[:, None])).astype(jnp.int32), axis=1)
    return pl.pallas_call(
        dense_kernel,
        out_shape=(
            pltpu.HBM((nodes, rows), BF16),
            jax.ShapeDtypeStruct((nodes // C, width), F32),
            jax.ShapeDtypeStruct((nodes // C, width), F32),
        ),
        in_specs=[pl.BlockSpec(memory_space=pltpu.SMEM)] * 6
        + [pl.BlockSpec(memory_space=pl.ANY), pl.BlockSpec(memory_space=pltpu.VMEM)],
        out_specs=(
            pl.BlockSpec(memory_space=pl.ANY),
            pl.BlockSpec(memory_space=pltpu.VMEM),
            pl.BlockSpec(memory_space=pltpu.VMEM),
        ),
        scratch_shapes=[
            pltpu.VMEM(blocks.shape, BF16),
            pltpu.VMEM((nodes, rows), BF16),
            pltpu.SemaphoreType.DMA((1 + QUARTERS,)),
        ],
        compiler_params=pltpu.CompilerParams(vmem_limit_bytes=20 * MIB),
        name="dense",
    )(
        order,
        node,
        lane,
        keep,
        bound,
        x.reshape(1),
        pltpu.with_memory_space_constraint(blocks, pltpu.HBM),
        probe,
    )


def chol_kernel(a_ref, upper_ref, inv_ref, *, root):
    n = a_ref.shape[0]
    groups = n // 8
    block = 8
    lane = lax.broadcasted_iota(jnp.int32, (8, n), 1)
    sub = lax.broadcasted_iota(jnp.int32, (8, n), 0)
    a = [a_ref[g * 8 : g * 8 + 8, :] for g in range(groups)]
    x = [(lane == sub + g * 8).astype(F32) for g in range(groups)]

    def row(value, i):
        return jnp.broadcast_to(value[i : i + 1, :], (8, n))

    def column(value, k):
        return jnp.broadcast_to(value[:, k : k + 1], (8, n))

    for k in range(0, n, block):
        g0, s = divmod(k, 8)
        cols = [column(a[g0], k + j) for j in range(block)]
        m = [[row(cols[j], s + i) for j in range(i + 1)] for i in range(block)]
        ra = [row(a[g0], s + i) for i in range(block)]
        rx = [row(x[g0], s + i) for i in range(block)]
        low = {}
        for j in range(block):
            one = 1.0 / m[j][j]
            for i in range(j + 1, block):
                low[i, j] = m[i][j] * one
                for h in range(j + 1, i + 1):
                    m[i][h] = m[i][h] - low[i, j] * m[h][j]
                ra[i] = ra[i] - low[i, j] * ra[j]
                rx[i] = rx[i] - low[i, j] * rx[j]
            ra[j], rx[j] = ra[j] * one, rx[j] * one
        for g in range(g0, groups):
            if g > g0:
                cols = [column(a[g], k + j) for j in range(block)]
            c = list(cols)
            for j in range(block):
                for h in range(j):
                    c[j] = c[j] - c[h] * low[j, h]
            if g == g0:
                c = [jnp.where(sub > s + j, c[j], 0.0) for j in range(block)]
            for j in range(block):
                a[g] = a[g] - c[j] * ra[j]
                x[g] = x[g] - c[j] * rx[j]
    for g in range(groups):
        own = lane == sub + g * 8
        diag = jnp.sum(jnp.where(own, a[g], 0.0), axis=1, keepdims=True)
        inv_root = 1.0 / jnp.sqrt(diag)
        upper_ref[g * 8 : g * 8 + 8, :] = jnp.where(
            lane >= sub + g * 8, a[g] * (inv_root / root), 0.0
        )
        inv_ref[g * 8 : g * 8 + 8, :] = x[g] * inv_root


def factor(gram, root):
    shape = jax.ShapeDtypeStruct(gram.shape, F32)
    return pl.pallas_call(
        functools.partial(chol_kernel, root=root),
        out_shape=(shape, shape),
        compiler_params=pltpu.CompilerParams(vmem_limit_bytes=8 * MIB),
        name="factor",
    )(gram)


def two_parts(value):
    high = value.astype(BF16)
    low = (value - high.astype(F32)).astype(BF16)
    return jnp.concatenate([high, low], axis=1)


def near_kernel(z_ref, out_ref, sem):
    copy = pltpu.make_async_copy(z_ref, out_ref, sem)
    copy.start()
    copy.wait()


def near(dense_z):
    return pl.pallas_call(
        near_kernel,
        out_shape=pltpu.VMEM(dense_z.shape, dense_z.dtype),
        in_specs=[pl.BlockSpec(memory_space=pl.ANY)],
        out_specs=pl.BlockSpec(memory_space=pltpu.VMEM),
        scratch_shapes=[pltpu.SemaphoreType.DMA],
        compiler_params=pltpu.CompilerParams(vmem_limit_bytes=MIB),
        cost_estimate=pl.CostEstimate(
            flops=0, bytes_accessed=2 * dense_z.size * 2, transcendentals=0
        ),
        name="near",
    )(pltpu.with_memory_space_constraint(dense_z, pltpu.HBM))


def node_kernel(x_ref, z_ref, *refs):
    c_refs, (mine_ref, other_ref, image_ref, both) = refs[:-4], refs[-4:]
    count = len(c_refs)
    size = image_ref.shape[0] // count
    for m in range(count):
        total = None
        for k, c_ref in enumerate(c_refs):
            code = c_ref[(m - k) % count].astype(jnp.int32).astype(F32)
            term = code[:size] * jnp.exp2(code[size : size + 1] - 14.0)
            total = term if total is None else total + term
        at = slice(m * size, (m + 1) * size)
        image_ref[at, :] = total
        both[at, :] = two_parts(total)
    node_loop(z_ref, both, x_ref[0], mine_ref, other_ref)


def node_sums(dense_z, codes, x):
    nodes, rows = dense_z.shape
    width = codes[0].shape[-1]
    half = jax.ShapeDtypeStruct((nodes // C, width), F32)
    vmem = pl.BlockSpec(memory_space=pltpu.VMEM)
    return pl.pallas_call(
        node_kernel,
        out_shape=(half, half, jax.ShapeDtypeStruct((rows, width), F32)),
        in_specs=[pl.BlockSpec(memory_space=pltpu.SMEM)] + [vmem] * (1 + len(codes)),
        out_specs=(vmem, vmem, vmem),
        scratch_shapes=[pltpu.VMEM((rows, 2 * width), BF16)],
        compiler_params=pltpu.CompilerParams(vmem_limit_bytes=8 * MIB),
        name="node_sums",
    )(x.reshape(1), pltpu.with_memory_space_constraint(dense_z, pltpu.VMEM), *codes)


def image_kernel(x_ref, z_ref, *refs, nbk):
    w_refs, (out_ref, acc) = refs[:-2], refs[-2:]
    width = out_ref.shape[1]
    for step, w_ref in enumerate(w_refs):
        if w_ref.dtype == BF16:
            w = w_ref[...].reshape(TILE, width)
        else:
            parts = []
            for piece in range(TILE // nbk):
                code = w_ref[piece].astype(jnp.int32).astype(F32)
                parts.append(code[:nbk] * jnp.exp2(code[nbk : nbk + 1] - 14.0))
            w = two_parts(jnp.concatenate(parts, axis=0))
        z = z_ref[pl.ds(block_of(x_ref[0], step), TILE), :]
        prod = lax.dot_general(w, z, (((0,), (0,)), ((), ())), preferred_element_type=F32)
        if step == 0:
            acc[...] = prod
        else:
            acc[...] += prod
    total = acc[:width, :]
    for i in range(width, acc.shape[0], width):
        total = total + acc[i : i + width, :]
    out_ref[...] = total.T


def image_part(dense_z, weights, x, nbk):
    rows = dense_z.shape[1]
    width = weights[0].shape[2]
    parts = 1 if weights[0].dtype == BF16 else 2
    return pl.pallas_call(
        functools.partial(image_kernel, nbk=nbk),
        out_shape=jax.ShapeDtypeStruct((rows, width), F32),
        in_specs=[
            pl.BlockSpec(memory_space=pltpu.SMEM),
        ]
        + [pl.BlockSpec(memory_space=pltpu.VMEM)] * (1 + len(weights)),
        out_specs=pl.BlockSpec(memory_space=pltpu.VMEM),
        scratch_shapes=[pltpu.VMEM((parts * width, rows), F32)],
        compiler_params=pltpu.CompilerParams(vmem_limit_bytes=8 * MIB),
        name="image_part",
    )(x.reshape(1), pltpu.with_memory_space_constraint(dense_z, pltpu.VMEM), *weights)


def along(axis, k):
    pairs = []
    for s in range(X * Z * C):
        x, z, c = s // (Z * C), s // C % Z, s % C
        if axis == "x":
            x = (x + k) % X
        if axis == "z":
            z = (z + k) % Z
        if axis == "c":
            c = (c + k) % C
        pairs.append((s, (x * Z + z) * C + c))
    return pairs


def from_core(value):
    return lax.ppermute(value, "sample", along("c", 1))


def exchange(value):
    groups = {}
    for device in range(X * Z * C):
        groups.setdefault((device // (Z * C), device % C), []).append(device)
    return lax.all_to_all(
        value,
        "sample",
        split_axis=0,
        concat_axis=0,
        axis_index_groups=list(groups.values()),
        tiled=True,
    )


def coded(value):
    top = jnp.max(jnp.abs(value), axis=1, keepdims=True)
    power = jnp.floor(jnp.log2(jnp.maximum(top, 1e-30))) + 1.0
    power = jnp.clip(power, -100.0, 127.0)
    return value * jnp.exp2(14.0 - power), power


def whole(value):
    return jnp.round(value).astype(I16)


def decoded(code, power):
    return code.astype(F32) * jnp.exp2(power.astype(F32) - 14.0)


def message(value, gram, multiple=8):
    scaled, power = coded(value)
    rows = [whole(scaled), power.astype(I16)]
    if gram is not None:
        scaled, power = coded(gram)
        high = jnp.round(scaled)
        rows += [high.astype(I16), whole((scaled - high) * 2.0**14), power.astype(I16)]
    rows = jnp.concatenate(rows, axis=1)
    return jnp.pad(rows, ((0, 0), (0, -rows.shape[1] % multiple), (0, 0)))


def read_value(rows, own):
    return decoded(rows[:, :own], rows[:, own : own + 1])


def read_gram(rows, own, lines):
    at = own + 1
    code = rows[:, at : at + lines].astype(F32)
    code = code + rows[:, at + lines : at + 2 * lines].astype(F32) * 2.0**-14
    return decoded(code, rows[:, at + 2 * lines : at + 2 * lines + 1])


def sum_nodes(mine, gram, others):
    width = mine.shape[1]
    lines = width // (X * Z)
    mine = mine.reshape(X, -1, width)
    rows = mine.shape[1]
    extra = None if gram is None else gram.reshape(X, -1, width)
    sent = message(mine[1:], None if gram is None else extra[1:])
    got = [lax.ppermute(sent[k - 1], "sample", along("x", k)) for k in range(1, X)]
    total = mine[0] + sum(read_value(part[None], rows)[0] for part in got)
    if gram is not None:
        gram = extra[0] + sum(read_gram(part[None], rows, Z * lines)[0] for part in got)
        gram = gram.reshape(Z, lines, width)
    sent = message(total.reshape(Z, -1, width), gram)
    sent, others = lax.optimization_barrier((sent, others))
    got = exchange(sent.reshape(-1, width))
    got, others = lax.optimization_barrier((got, others))
    got = got.reshape(Z, -1, width)
    if gram is not None:
        gram = jnp.sum(read_gram(got, rows // Z, lines), axis=0)
    return jnp.sum(read_value(got, rows // Z), axis=0), gram, others


def spread(own, dense_z, others):
    copies = jnp.broadcast_to(own[None], (Z,) + own.shape).reshape(-1, own.shape[1])
    copies, others = lax.optimization_barrier((copies, others))
    got = exchange(copies)
    got, dense_z, others = lax.optimization_barrier((got, dense_z, others))
    got = got.reshape((Z,) + own.shape)
    mine = [lax.ppermute(got, "sample", along("x", -k)) for k in range(1, X)]
    mine, near_z = lax.optimization_barrier((mine, near(dense_z)))
    mine = [got] + mine
    return mine + [from_core(part) for part in mine], near_z, others


def scatter_interval(value, ny):
    pieces = value.reshape(ny, -1, value.shape[1])
    rows = pieces.shape[1]
    sent = message(pieces[1:], None)
    total = pieces[0]
    for k in range(1, ny):
        got = lax.ppermute(sent[k - 1], "interval", [(i, (i + k) % ny) for i in range(ny)])
        total = total + read_value(got[None], rows)[0]
    return total


def gather_interval(value, ny):
    parts = [value]
    for k in range(1, ny):
        parts.append(lax.ppermute(value, "interval", [(i, (i - k) % ny) for i in range(ny)]))
    return parts


def split(value, count):
    parts = []
    for _ in range(count):
        part = lax.reduce_precision(value, exponent_bits=8, mantissa_bits=7)
        value = value - part
        parts.append(part.astype(BF16))
    return jnp.concatenate(parts, axis=1)


def gram_of(image):
    return lax.dot_general(
        image, image, (((0,), (0,)), ((), ())), precision=HIGH, preferred_element_type=F32
    )


def shards(
    probes, lengths, incidence, block_rows, block_cols, block_count, tree_sample, tree_position
):
    ndev = lax.axis_size("sample")
    ny = lax.axis_size("interval")
    mine = lax.axis_index("sample")
    iy = lax.axis_index("interval")
    rows_here, width = probes.shape
    samples = rows_here * ndev
    root = math.sqrt(samples)
    share = rows_here // ndev
    quarter = rows_here // ny
    blocks = incidence[0]
    slots, nbk, sb = blocks.shape
    nodes = ndev * nbk
    nrow = rows_here // sb
    turn = nrow // ny

    at = jnp.arange(rows_here, dtype=jnp.int32)
    rank = jnp.sum((tree_position[None, :] < tree_position[:, None]).astype(jnp.int32), axis=1)
    to_send = (at[:, None] == rank[None, :]).astype(BF16)
    sent = jnp.dot(to_send, probes, preferred_element_type=F32).astype(BF16)
    moved = lax.all_to_all(sent, "sample", split_axis=0, concat_axis=0, tiled=True)

    source = tree_sample // rows_here
    same = (source[None, :] == source[:, None]) & (at[None, :] < at[:, None])
    order = jnp.sum(same.astype(jnp.int32), axis=1)
    source = jnp.roll(source, -iy * quarter)
    order = jnp.roll(order, -iy * quarter)
    slot = source * share + order
    rows = block_rows[0]
    cols = block_cols[0]
    row_at = (rows + nrow - iy * turn) % nrow
    col_at = ((cols + mine) % C) * (ndev // C) + cols // C
    own_lens = lax.dynamic_slice_in_dim(lengths[0], mine * nbk, nbk, 0)

    def scale(owned):
        return own_lens[:, None] * owned / samples

    here = mine // (Z * C)
    col_at, own_lens = lax.optimization_barrier((col_at, own_lens))
    from_moved = (slot[:, None] == at[None, :]).astype(BF16)
    tree_probe = jnp.dot(from_moved, moved, preferred_element_type=F32).astype(BF16)
    dense_z, first, second = dense(
        blocks, row_at, col_at, block_count[0], tree_probe, here, nodes
    )
    tied = (own_lens, rank, source, order, here)
    owned, _, tied = sum_nodes(first + from_core(second), None, tied)
    own_lens = tied[0]
    weights, near_z, tied = spread(scale(owned).astype(BF16), dense_z, tied)
    own_lens, here = tied[0], tied[4]
    part = image_part(near_z, weights, here, nbk)
    code = message(part.reshape(ny, quarter, width), None, 16)
    code, far_z = lax.optimization_barrier((code, dense_z))
    codes = gather_interval(code, ny)

    first, second, image = node_sums(near(far_z), codes, here)
    second = from_core(second)
    gram = gram_of(image)
    lines = width // (X * Z)
    gram = jnp.roll(gram, -here * (Z * lines), axis=0)
    owned, gram, tied = sum_nodes(first + second, gram, tied)
    own_lens = tied[0]
    sent = message(scale(owned)[None], gram[None], 16)[0]
    weights, near_z, tied = spread(sent, dense_z, tied)
    rank, source, order, here = tied[1:]
    part = image_part(near_z, weights, here, nbk)
    part, weights, here = lax.optimization_barrier((part, weights, here))
    gram = [read_gram(got, nbk, lines).reshape(-1, width) for got in weights]
    gram = jnp.concatenate([gram[k] + gram[X + k] for k in range(X)], axis=0)
    gram = jnp.roll(gram, here * (Z * lines), axis=0)
    lines = width // ndev
    _, inverse = factor(gram, root)

    per = share // ny
    jrel = (order // per + ny - iy) % ny
    goal = jrel * quarter + source * per + order % per
    to_goal = (at[:, None] == goal[None, :]).astype(BF16)
    pieces = jnp.dot(to_goal, split(part, 3), preferred_element_type=F32)
    part = pieces[:, :width] + pieces[:, width : 2 * width] + pieces[:, 2 * width :]
    image = scatter_interval(part, ny)
    image = root * jnp.dot(image, inverse.T, precision=HIGH, preferred_element_type=F32)
    gram = gram_of(image).reshape(ndev, -1, width)
    image = jnp.concatenate([image.reshape(ndev, per, width), gram], axis=1)
    image = jnp.pad(image, ((0, 0), (0, -image.shape[1] % 8), (0, 0)))
    image, rank, iy = lax.optimization_barrier((image, rank, iy))
    image = lax.all_to_all(
        image.reshape(-1, width), "sample", split_axis=0, concat_axis=0, tiled=True
    )
    image, rank, iy = lax.optimization_barrier((image, rank, iy))
    image = image.reshape(ndev, -1, width)
    gram = jnp.sum(image[:, per : per + lines], axis=0)
    image = image[:, :per].reshape(quarter, width)
    image = jnp.stack(gather_interval(message(image[None], gram[None])[0], ny))
    gram = jnp.sum(read_gram(image, quarter, lines), axis=0)
    image = read_value(image, quarter).reshape(rows_here, width)
    k = rank % share
    back = ((k // per + ny - iy) % ny) * quarter + (rank // share) * per + k % per
    from_goal = (back[:, None] == at[None, :]).astype(BF16)
    pieces = jnp.dot(from_goal, split(image, 2), preferred_element_type=F32)
    image = pieces[:, :width] + pieces[:, width:]
    gram = jnp.broadcast_to(gram[None], (ndev,) + gram.shape).reshape(-1, width)
    gram, image = lax.optimization_barrier((gram, image))
    gram = lax.all_to_all(gram, "sample", split_axis=0, concat_axis=0, tiled=True)
    gram, image = lax.optimization_barrier((gram, image))
    upper, inverse = factor(gram, root)
    basis = root * jnp.dot(image, inverse.T, precision=HIGH, preferred_element_type=F32)
    return (basis, upper)


def solution(mesh):
    in_specs = (
        P("sample", None),
        P("interval", None),
        P("interval", "sample", None, None),
        P("interval", "sample"),
        P("interval", "sample"),
        P("interval", "sample"),
        P("sample"),
        P("sample"),
    )
    out_specs = (P("sample", None), P())
    return jax.shard_map(shards, mesh=mesh, in_specs=in_specs, out_specs=out_specs, check_vma=False)
```

```python
import functools
import math

import jax
import jax.numpy as jnp
from jax import lax
from jax.experimental import pallas as pl
from jax.experimental.pallas import tpu as pltpu
from jax.sharding import PartitionSpec as P

ITERS = 2
X, Z, C = 4, 8, 2
HIGH = lax.Precision.HIGHEST
F32 = jnp.float32
BF16 = jnp.bfloat16
MIB = 1024 * 1024
I16 = jnp.int16
TILE = 512
QUARTERS = 4


def block_of(x, k):
    return pl.multiple_of((k // X * X + lax.rem(x + k % X, X)) * TILE, TILE)


def node_loop(z_ref, p_ref, x, mine_ref, other_ref):
    width = mine_ref.shape[1]
    for k in range(C * X):
        z = z_ref[pl.ds(block_of(x, k), TILE), :]
        prod = jnp.dot(z, p_ref[...], preferred_element_type=F32)
        total = prod[:, :width]
        if prod.shape[1] > width:
            total = total + prod[:, width:]
        to_ref = mine_ref if k < X else other_ref
        to_ref[k % X * TILE : (k % X + 1) * TILE, :] = total


def dense_kernel(
    order_ref, node_ref, lane_ref, keep_ref, bound_ref, x_ref, blk_ref, p_ref,
    out_ref, mine_ref, other_ref, held, z, sem,
):
    nodes, rows = z.shape
    nbk, sb = held.shape[1:]
    tile = 128
    copy = pltpu.make_async_copy(blk_ref, held, sem.at[0])
    copy.start()

    def zero(i, carry):
        z[pl.ds(pl.multiple_of(i * tile, tile), tile), :] = jnp.zeros((tile, rows), BF16)
        return carry

    lax.fori_loop(0, nodes // tile, zero, 0)
    copy.wait()

    def add(i, total):
        total = jnp.where(keep_ref[i] == 1, total, 0.0) + held[order_ref[i]].astype(F32)
        node = pl.multiple_of(node_ref[i], nbk)
        lane = pl.multiple_of(lane_ref[i], sb)
        z[pl.ds(node, nbk), pl.ds(lane, sb)] = total.astype(BF16)
        return total

    unroll = 8
    total = jnp.zeros((nbk, sb), F32)
    part = nodes // QUARTERS
    backs = []
    for q in range(QUARTERS):
        first = 0 if q == 0 else bound_ref[q - 1]
        last = bound_ref[q]
        turns = (last - first) // unroll

        def several(i, total, first=first):
            for j in range(unroll):
                total = add(first + i * unroll + j, total)
            return total

        total = lax.fori_loop(0, turns, several, total)
        total = lax.fori_loop(first + turns * unroll, last, add, total)
        at = pl.ds(q * part, part)
        backs.append(pltpu.make_async_copy(z.at[at], out_ref.at[at], sem.at[1 + q]))
        backs[-1].start()
    node_loop(z, p_ref, x_ref[0], mine_ref, other_ref)
    for back in backs:
        back.wait()


def dense(blocks, row_at, col_at, count, probe, x, nodes):
    slots, nbk, sb = blocks.shape
    rows, width = probe.shape
    nrow = rows // sb
    place = col_at * nrow + row_at
    at = jnp.arange(slots, dtype=jnp.int32)
    live = at < count[0]
    key = jnp.where(live, place * slots, nodes * rows) + at
    rank = jnp.sum((key[None, :] < key[:, None]).astype(jnp.int32), axis=1)
    earlier = (place[None, :] == place[:, None]) & (at[None, :] < at[:, None])
    keep = jnp.max(earlier.astype(jnp.int32), axis=1)
    hit = rank[None, :] == at[:, None]
    order, node, lane, keep = [
        jnp.sum(jnp.where(hit, value[None, :], 0), axis=1)
        for value in (at, col_at * nbk, row_at * sb, keep)
    ]
    ends = (jnp.arange(QUARTERS, dtype=jnp.int32) + 1) * (nodes // nbk * nrow // QUARTERS)
    bound = jnp.sum((live & (place < ends[:, None])).astype(jnp.int32), axis=1)
    return pl.pallas_call(
        dense_kernel,
        out_shape=(
            pltpu.HBM((nodes, rows), BF16),
            jax.ShapeDtypeStruct((nodes // C, width), F32),
            jax.ShapeDtypeStruct((nodes // C, width), F32),
        ),
        in_specs=[pl.BlockSpec(memory_space=pltpu.SMEM)] * 6
        + [pl.BlockSpec(memory_space=pl.ANY), pl.BlockSpec(memory_space=pltpu.VMEM)],
        out_specs=(
            pl.BlockSpec(memory_space=pl.ANY),
            pl.BlockSpec(memory_space=pltpu.VMEM),
            pl.BlockSpec(memory_space=pltpu.VMEM),
        ),
        scratch_shapes=[
            pltpu.VMEM(blocks.shape, BF16),
            pltpu.VMEM((nodes, rows), BF16),
            pltpu.SemaphoreType.DMA((1 + QUARTERS,)),
        ],
        compiler_params=pltpu.CompilerParams(vmem_limit_bytes=20 * MIB),
        name="dense",
    )(
        order,
        node,
        lane,
        keep,
        bound,
        x.reshape(1),
        pltpu.with_memory_space_constraint(blocks, pltpu.HBM),
        probe,
    )


def chol_kernel(a_ref, upper_ref, inv_ref, *, root):
    n = a_ref.shape[0]
    groups = n // 8
    block = 8
    lane = lax.broadcasted_iota(jnp.int32, (8, n), 1)
    sub = lax.broadcasted_iota(jnp.int32, (8, n), 0)
    a = [a_ref[g * 8 : g * 8 + 8, :] for g in range(groups)]
    x = [(lane == sub + g * 8).astype(F32) for g in range(groups)]

    def row(value, i):
        return jnp.broadcast_to(value[i : i + 1, :], (8, n))

    def column(value, k):
        return jnp.broadcast_to(value[:, k : k + 1], (8, n))

    for k in range(0, n, block):
        g0, s = divmod(k, 8)
        cols = [column(a[g0], k + j) for j in range(block)]
        m = [[row(cols[j], s + i) for j in range(i + 1)] for i in range(block)]
        ra = [row(a[g0], s + i) for i in range(block)]
        rx = [row(x[g0], s + i) for i in range(block)]
        low = {}
        for j in range(block):
            one = 1.0 / m[j][j]
            for i in range(j + 1, block):
                low[i, j] = m[i][j] * one
                for h in range(j + 1, i + 1):
                    m[i][h] = m[i][h] - low[i, j] * m[h][j]
                ra[i] = ra[i] - low[i, j] * ra[j]
                rx[i] = rx[i] - low[i, j] * rx[j]
            ra[j], rx[j] = ra[j] * one, rx[j] * one
        for g in range(g0, groups):
            if g > g0:
                cols = [column(a[g], k + j) for j in range(block)]
            c = list(cols)
            for j in range(block):
                for h in range(j):
                    c[j] = c[j] - c[h] * low[j, h]
            if g == g0:
                c = [jnp.where(sub > s + j, c[j], 0.0) for j in range(block)]
            for j in range(block):
                a[g] = a[g] - c[j] * ra[j]
                x[g] = x[g] - c[j] * rx[j]
    for g in range(groups):
        own = lane == sub + g * 8
        diag = jnp.sum(jnp.where(own, a[g], 0.0), axis=1, keepdims=True)
        inv_root = 1.0 / jnp.sqrt(diag)
        upper_ref[g * 8 : g * 8 + 8, :] = jnp.where(
            lane >= sub + g * 8, a[g] * (inv_root / root), 0.0
        )
        inv_ref[g * 8 : g * 8 + 8, :] = x[g] * inv_root


def factor(gram, root):
    shape = jax.ShapeDtypeStruct(gram.shape, F32)
    return pl.pallas_call(
        functools.partial(chol_kernel, root=root),
        out_shape=(shape, shape),
        compiler_params=pltpu.CompilerParams(vmem_limit_bytes=8 * MIB),
        cost_estimate=pl.CostEstimate(
            flops=2 * gram.size * gram.shape[0], bytes_accessed=16 * MIB, transcendentals=0
        ),
        name="factor",
    )(gram)


def two_parts(value):
    high = value.astype(BF16)
    low = (value - high.astype(F32)).astype(BF16)
    return jnp.concatenate([high, low], axis=1)


def near_kernel(z_ref, out_ref, sem):
    copy = pltpu.make_async_copy(z_ref, out_ref, sem)
    copy.start()
    copy.wait()


def near(dense_z):
    return pl.pallas_call(
        near_kernel,
        out_shape=pltpu.VMEM(dense_z.shape, dense_z.dtype),
        in_specs=[pl.BlockSpec(memory_space=pl.ANY)],
        out_specs=pl.BlockSpec(memory_space=pltpu.VMEM),
        scratch_shapes=[pltpu.SemaphoreType.DMA],
        compiler_params=pltpu.CompilerParams(vmem_limit_bytes=MIB),
        cost_estimate=pl.CostEstimate(
            flops=0, bytes_accessed=2 * dense_z.size * 2, transcendentals=0
        ),
        name="near",
    )(pltpu.with_memory_space_constraint(dense_z, pltpu.HBM))


def node_kernel(x_ref, z_ref, *refs):
    c_refs, (mine_ref, other_ref, image_ref, both) = refs[:-4], refs[-4:]
    count = len(c_refs)
    size = image_ref.shape[0] // count
    for m in range(count):
        total = None
        for k, c_ref in enumerate(c_refs):
            code = c_ref[(m - k) % count].astype(jnp.int32).astype(F32)
            term = code[:size] * jnp.exp2(code[size : size + 1] - 14.0)
            total = term if total is None else total + term
        at = slice(m * size, (m + 1) * size)
        image_ref[at, :] = total
        both[at, :] = two_parts(total)
    node_loop(z_ref, both, x_ref[0], mine_ref, other_ref)


def node_sums(dense_z, codes, x):
    nodes, rows = dense_z.shape
    width = codes[0].shape[-1]
    half = jax.ShapeDtypeStruct((nodes // C, width), F32)
    vmem = pl.BlockSpec(memory_space=pltpu.VMEM)
    return pl.pallas_call(
        node_kernel,
        out_shape=(half, half, jax.ShapeDtypeStruct((rows, width), F32)),
        in_specs=[pl.BlockSpec(memory_space=pltpu.SMEM)] + [vmem] * (1 + len(codes)),
        out_specs=(vmem, vmem, vmem),
        scratch_shapes=[pltpu.VMEM((rows, 2 * width), BF16)],
        compiler_params=pltpu.CompilerParams(vmem_limit_bytes=8 * MIB),
        name="node_sums",
    )(x.reshape(1), pltpu.with_memory_space_constraint(dense_z, pltpu.VMEM), *codes)


def image_kernel(x_ref, z_ref, *refs, nbk):
    w_refs, (out_ref, acc) = refs[:-2], refs[-2:]
    width = out_ref.shape[1]
    for step, w_ref in enumerate(w_refs):
        if w_ref.dtype == BF16:
            w = w_ref[...].reshape(TILE, width)
        else:
            parts = []
            for piece in range(TILE // nbk):
                code = w_ref[piece].astype(jnp.int32).astype(F32)
                parts.append(code[:nbk] * jnp.exp2(code[nbk : nbk + 1] - 14.0))
            w = two_parts(jnp.concatenate(parts, axis=0))
        z = z_ref[pl.ds(block_of(x_ref[0], step), TILE), :]
        prod = lax.dot_general(w, z, (((0,), (0,)), ((), ())), preferred_element_type=F32)
        if step == 0:
            acc[...] = prod
        else:
            acc[...] += prod
    total = acc[:width, :]
    for i in range(width, acc.shape[0], width):
        total = total + acc[i : i + width, :]
    out_ref[...] = total.T


def image_part(dense_z, weights, x, nbk):
    rows = dense_z.shape[1]
    width = weights[0].shape[2]
    parts = 1 if weights[0].dtype == BF16 else 2
    return pl.pallas_call(
        functools.partial(image_kernel, nbk=nbk),
        out_shape=jax.ShapeDtypeStruct((rows, width), F32),
        in_specs=[
            pl.BlockSpec(memory_space=pltpu.SMEM),
        ]
        + [pl.BlockSpec(memory_space=pltpu.VMEM)] * (1 + len(weights)),
        out_specs=pl.BlockSpec(memory_space=pltpu.VMEM),
        scratch_shapes=[pltpu.VMEM((parts * width, rows), F32)],
        compiler_params=pltpu.CompilerParams(vmem_limit_bytes=8 * MIB),
        name="image_part",
    )(x.reshape(1), pltpu.with_memory_space_constraint(dense_z, pltpu.VMEM), *weights)


def along(axis, k):
    pairs = []
    for s in range(X * Z * C):
        x, z, c = s // (Z * C), s // C % Z, s % C
        if axis == "x":
            x = (x + k) % X
        if axis == "z":
            z = (z + k) % Z
        if axis == "c":
            c = (c + k) % C
        pairs.append((s, (x * Z + z) * C + c))
    return pairs


def from_core(value):
    return lax.ppermute(value, "sample", along("c", 1))


def exchange(value):
    groups = {}
    for device in range(X * Z * C):
        groups.setdefault((device // (Z * C), device % C), []).append(device)
    return lax.all_to_all(
        value,
        "sample",
        split_axis=0,
        concat_axis=0,
        axis_index_groups=list(groups.values()),
        tiled=True,
    )


def coded(value):
    top = jnp.max(jnp.abs(value), axis=1, keepdims=True)
    power = jnp.floor(jnp.log2(jnp.maximum(top, 1e-30))) + 1.0
    power = jnp.clip(power, -100.0, 127.0)
    return value * jnp.exp2(14.0 - power), power


def whole(value):
    return jnp.round(value).astype(I16)


def decoded(code, power):
    return code.astype(F32) * jnp.exp2(power.astype(F32) - 14.0)


def message(value, gram, multiple=8):
    scaled, power = coded(value)
    rows = [whole(scaled), power.astype(I16)]
    if gram is not None:
        scaled, power = coded(gram)
        high = jnp.round(scaled)
        rows += [high.astype(I16), whole((scaled - high) * 2.0**14), power.astype(I16)]
    rows = jnp.concatenate(rows, axis=1)
    return jnp.pad(rows, ((0, 0), (0, -rows.shape[1] % multiple), (0, 0)))


def read_value(rows, own):
    return decoded(rows[:, :own], rows[:, own : own + 1])


def read_gram(rows, own, lines):
    at = own + 1
    code = rows[:, at : at + lines].astype(F32)
    code = code + rows[:, at + lines : at + 2 * lines].astype(F32) * 2.0**-14
    return decoded(code, rows[:, at + 2 * lines : at + 2 * lines + 1])


def sum_nodes(mine, gram, others):
    width = mine.shape[1]
    lines = width // (X * Z)
    mine = mine.reshape(X, -1, width)
    rows = mine.shape[1]
    extra = None if gram is None else gram.reshape(X, -1, width)
    sent = message(mine[1:], None if gram is None else extra[1:])
    got = [lax.ppermute(sent[k - 1], "sample", along("x", k)) for k in range(1, X)]
    total = mine[0] + sum(read_value(part[None], rows)[0] for part in got)
    if gram is not None:
        gram = extra[0] + sum(read_gram(part[None], rows, Z * lines)[0] for part in got)
        gram = gram.reshape(Z, lines, width)
    sent = message(total.reshape(Z, -1, width), gram)
    sent, others = lax.optimization_barrier((sent, others))
    got = exchange(sent.reshape(-1, width))
    got, others = lax.optimization_barrier((got, others))
    got = got.reshape(Z, -1, width)
    if gram is not None:
        gram = jnp.sum(read_gram(got, rows // Z, lines), axis=0)
    return jnp.sum(read_value(got, rows // Z), axis=0), gram, others


def spread(own, dense_z, others):
    copies = jnp.broadcast_to(own[None], (Z,) + own.shape).reshape(-1, own.shape[1])
    copies, others = lax.optimization_barrier((copies, others))
    got = exchange(copies)
    got, dense_z, others = lax.optimization_barrier((got, dense_z, others))
    got = got.reshape((Z,) + own.shape)
    mine = [lax.ppermute(got, "sample", along("x", -k)) for k in range(1, X)]
    mine, near_z = lax.optimization_barrier((mine, near(dense_z)))
    mine = [got] + mine
    return mine + [from_core(part) for part in mine], near_z, others


def scatter_interval(value, ny):
    pieces = value.reshape(ny, -1, value.shape[1])
    rows = pieces.shape[1]
    sent = message(pieces[1:], None)
    total = pieces[0]
    for k in range(1, ny):
        got = lax.ppermute(sent[k - 1], "interval", [(i, (i + k) % ny) for i in range(ny)])
        total = total + read_value(got[None], rows)[0]
    return total


def gather_interval(value, ny):
    parts = [value]
    for k in range(1, ny):
        parts.append(lax.ppermute(value, "interval", [(i, (i - k) % ny) for i in range(ny)]))
    return parts


def split(value, count):
    parts = []
    for _ in range(count):
        part = lax.reduce_precision(value, exponent_bits=8, mantissa_bits=7)
        value = value - part
        parts.append(part.astype(BF16))
    return jnp.concatenate(parts, axis=1)


def gram_of(image):
    return lax.dot_general(
        image, image, (((0,), (0,)), ((), ())), precision=HIGH, preferred_element_type=F32
    )


def shards(
    probes, lengths, incidence, block_rows, block_cols, block_count, tree_sample, tree_position
):
    ndev = lax.axis_size("sample")
    ny = lax.axis_size("interval")
    mine = lax.axis_index("sample")
    iy = lax.axis_index("interval")
    rows_here, width = probes.shape
    samples = rows_here * ndev
    root = math.sqrt(samples)
    share = rows_here // ndev
    quarter = rows_here // ny
    blocks = incidence[0]
    slots, nbk, sb = blocks.shape
    nodes = ndev * nbk
    nrow = rows_here // sb
    turn = nrow // ny

    at = jnp.arange(rows_here, dtype=jnp.int32)
    rank = jnp.sum((tree_position[None, :] < tree_position[:, None]).astype(jnp.int32), axis=1)
    to_send = (at[:, None] == rank[None, :]).astype(BF16)
    sent = jnp.dot(to_send, probes, preferred_element_type=F32).astype(BF16)
    moved = lax.all_to_all(sent, "sample", split_axis=0, concat_axis=0, tiled=True)

    source = tree_sample // rows_here
    same = (source[None, :] == source[:, None]) & (at[None, :] < at[:, None])
    order = jnp.sum(same.astype(jnp.int32), axis=1)
    source = jnp.roll(source, -iy * quarter)
    order = jnp.roll(order, -iy * quarter)
    slot = source * share + order
    rows = block_rows[0]
    cols = block_cols[0]
    row_at = (rows + nrow - iy * turn) % nrow
    col_at = ((cols + mine) % C) * (ndev // C) + cols // C
    own_lens = lax.dynamic_slice_in_dim(lengths[0], mine * nbk, nbk, 0)

    def scale(owned):
        return own_lens[:, None] * owned / samples

    here = mine // (Z * C)
    col_at, own_lens = lax.optimization_barrier((col_at, own_lens))
    from_moved = (slot[:, None] == at[None, :]).astype(BF16)
    tree_probe = jnp.dot(from_moved, moved, preferred_element_type=F32).astype(BF16)
    dense_z, first, second = dense(
        blocks, row_at, col_at, block_count[0], tree_probe, here, nodes
    )
    tied = (own_lens, rank, source, order, here)
    owned, _, tied = sum_nodes(first + from_core(second), None, tied)
    own_lens = tied[0]
    weights, near_z, tied = spread(scale(owned).astype(BF16), dense_z, tied)
    own_lens, here = tied[0], tied[4]
    part = image_part(near_z, weights, here, nbk)
    code = message(part.reshape(ny, quarter, width), None, 16)
    code, far_z = lax.optimization_barrier((code, dense_z))
    codes = gather_interval(code, ny)

    first, second, image = node_sums(near(far_z), codes, here)
    second = from_core(second)
    gram = gram_of(image)
    lines = width // (X * Z)
    gram = jnp.roll(gram, -here * (Z * lines), axis=0)
    owned, gram, tied = sum_nodes(first + second, gram, tied)
    own_lens = tied[0]
    sent = message(scale(owned)[None], gram[None], 16)[0]
    weights, near_z, tied = spread(sent, dense_z, tied)
    rank, source, order, here = tied[1:]
    part = image_part(near_z, weights, here, nbk)
    part, weights, here = lax.optimization_barrier((part, weights, here))
    gram = [read_gram(got, nbk, lines).reshape(-1, width) for got in weights]
    gram = jnp.concatenate([gram[k] + gram[X + k] for k in range(X)], axis=0)
    gram = jnp.roll(gram, here * (Z * lines), axis=0)
    lines = width // ndev
    _, inverse = factor(gram, root)

    per = share // ny
    jrel = (order // per + ny - iy) % ny
    goal = jrel * quarter + source * per + order % per
    to_goal = (at[:, None] == goal[None, :]).astype(BF16)
    pieces = jnp.dot(to_goal, split(part, 3), preferred_element_type=F32)
    part = pieces[:, :width] + pieces[:, width : 2 * width] + pieces[:, 2 * width :]
    image = scatter_interval(part, ny)
    image = root * jnp.dot(image, inverse.T, precision=HIGH, preferred_element_type=F32)
    gram = gram_of(image).reshape(ndev, -1, width)
    image = jnp.concatenate([image.reshape(ndev, per, width), gram], axis=1)
    image = jnp.pad(image, ((0, 0), (0, -image.shape[1] % 8), (0, 0)))
    image, rank, iy = lax.optimization_barrier((image, rank, iy))
    image = lax.all_to_all(
        image.reshape(-1, width), "sample", split_axis=0, concat_axis=0, tiled=True
    )
    image, rank, iy = lax.optimization_barrier((image, rank, iy))
    image = image.reshape(ndev, -1, width)
    gram = jnp.sum(image[:, per : per + lines], axis=0)
    image = image[:, :per].reshape(quarter, width)
    image = jnp.stack(gather_interval(message(image[None], gram[None])[0], ny))
    gram = jnp.sum(read_gram(image, quarter, lines), axis=0)
    image = read_value(image, quarter).reshape(rows_here, width)
    k = rank % share
    back = ((k // per + ny - iy) % ny) * quarter + (rank // share) * per + k % per
    from_goal = (back[:, None] == at[None, :]).astype(BF16)
    pieces = jnp.dot(from_goal, split(image, 2), preferred_element_type=F32)
    image = pieces[:, :width] + pieces[:, width:]
    gram = jnp.broadcast_to(gram[None], (ndev,) + gram.shape).reshape(-1, width)
    gram, image = lax.optimization_barrier((gram, image))
    gram = lax.all_to_all(gram, "sample", split_axis=0, concat_axis=0, tiled=True)
    gram, image = lax.optimization_barrier((gram, image))
    upper, inverse = factor(gram, root)
    basis = root * jnp.dot(image, inverse.T, precision=HIGH, preferred_element_type=F32)
    return (basis, upper)


def solution(mesh):
    in_specs = (
        P("sample", None),
        P("interval", None),
        P("interval", "sample", None, None),
        P("interval", "sample"),
        P("interval", "sample"),
        P("interval", "sample"),
        P("sample"),
        P("sample"),
    )
    out_specs = (P("sample", None), P())
    return jax.shard_map(shards, mesh=mesh, in_specs=in_specs, out_specs=out_specs, check_vma=False)
```
